256 devices in a mesh: chan: 32 (over z_lo, x, core), tm: 8 (over z_hi, y).
Axes of the slice: x: 4, y: 4, z: 8 (z_hi: 2, z_lo: 4; z = z_hi * 4 + z_lo), core: 2. Of those that a mesh axis runs over, the one named last changes fastest.
Arguments:
- traces: float32 [4096, 32768], P('chan', 'tm'), may hold values from -6 to 6
- offsets: int32 [32], P('tm'), may hold values from 0 to 4095, as said below
Outputs:
- stacks: float32 [4, 32, 4096, 128], P(None, None, ('chan', 'tm'))
The draws below stay inside these ranges and needn't reach their ends.
Inputs may be any that keep to these rules, and one draw needn't show every extreme that they name: `offsets`: every time segment but at most one has a window that starts in the last 1024 samples of its segment.
All inputs are finite; a program needn't handle non-finite values.
Results may differ from the reference program's by a relative error of at most 0.0019.
Values may be sent and summed in bfloat16 or wider, within the bound.
A program may use at most 128 MiB of HBM per device.

```python
import jax
import jax.numpy as jnp
from jax import lax

CH_DEV = 128
NFFT = 2048
BAND = 64
WIN_DEV = 4
SEG_DEV = 4096
ROUNDS = 4
NB = 16
CHANNELS = 4096
WINDOWS = 32
SAMPLES = 32768
N_CHAN = 32


def draw_offsets(key, part):
    key = jax.random.fold_in(key, 5)
    keys = jax.random.split(key, 5)
    groups = WINDOWS // WIN_DEV
    base = jax.random.randint(keys[0], (groups, WIN_DEV), 0, SEG_DEV)
    late = jax.random.randint(keys[1], (groups, 1), SEG_DEV - NFFT // 2, SEG_DEV)
    picked = jax.random.randint(keys[2], (groups, 1), 0, WIN_DEV)
    slots = jnp.arange(WIN_DEV, dtype=jnp.int32)[None, :]
    base = jnp.where(slots == picked, late, base).reshape(-1)
    index = jnp.arange(WINDOWS, dtype=jnp.int32)
    top = jax.random.randint(keys[3], (), 0, WINDOWS)
    bottom = (top + 1 + jax.random.randint(keys[4], (), 0, WINDOWS - 1)) % WINDOWS
    base = jnp.where(index == top, SEG_DEV - 1, base)
    base = jnp.where(index == bottom, 0, base)
    return base.astype(jnp.int32)


def shard_levels(key, dims, cuts, smallest, largest):
    def one(axis_at, parts):
        heights = jax.random.uniform(jax.random.fold_in(jax.random.fold_in(key, 6), axis_at), (parts,), jnp.float32, smallest / len(cuts), largest / len(cuts))
        return jnp.repeat(jnp.exp(heights), dims[axis_at] // parts).reshape((-1,) + (1,) * (len(dims) - axis_at - 1))

    loudness = one(*cuts[0])
    for cut in cuts[1:]:
        loudness = loudness * one(*cut)
    return loudness


def gaussian(rng, extent, deviation, bound, cuts=(), kind=jnp.bfloat16):
    loudness = shard_levels(rng, extent, cuts, -0.22, 0.18) if cuts else 1.0
    drawn = jax.random.normal(rng, extent, jnp.float32) * deviation * loudness
    return jnp.minimum(jnp.maximum(drawn, -bound), bound).astype(kind)


def setup_inputs(seed: int = 0) -> dict:
    splits = jax.random.split(jax.random.key(seed), 3)
    traces = gaussian(splits[0], (CHANNELS, SAMPLES), 1.0, 6.0, ((0, 32), (1, 8)), jnp.float32)
    offsets = draw_offsets(jax.random.fold_in(splits[2], 71), 0)
    return {"traces": traces, "offsets": offsets}


def whiten(segment):
    centered = segment - lax.optimization_barrier(jnp.mean(segment, axis=1, keepdims=True))
    normalized = centered * lax.rsqrt(lax.optimization_barrier(jnp.mean(centered * centered, axis=1, keepdims=True)) + 1e-06)
    spectrum = jnp.fft.rfft(normalized, axis=1)[:, :NFFT // 2]
    real_part = jnp.real(spectrum).astype(jnp.float32)
    imag_part = jnp.imag(spectrum).astype(jnp.float32)
    magnitude = jnp.sqrt(real_part * real_part + imag_part * imag_part)
    level = lax.optimization_barrier(jnp.mean(magnitude.reshape(-1, NB, BAND), axis=2, keepdims=True))
    factor = 1.0 / (level + 1e-06)
    white_real = real_part.reshape(-1, NB, BAND) * factor
    white_imag = imag_part.reshape(-1, NB, BAND) * factor
    return jnp.stack([white_real, white_imag], axis=1).astype(jnp.bfloat16)

def to_blocks(whitened):
    moved = jnp.transpose(whitened, (3, 1, 0, 2, 4))
    moved = moved.reshape(NB, N_CHAN, CH_DEV, WINDOWS * 2 * BAND)
    return jnp.transpose(moved, (1, 0, 2, 3))

def reference(traces, offsets):
    padded = jnp.pad(traces, ((0, 0), (0, NFFT)))
    starts = jnp.arange(WINDOWS, dtype=jnp.int32) // WIN_DEV * SEG_DEV + offsets.astype(jnp.int32)

    def one_window(start):
        return whiten(lax.dynamic_slice_in_dim(padded, start, NFFT, 1))
    whitened = lax.map(one_window, starts)
    twisted = jnp.stack([whitened[:, :, 1], -whitened[:, :, 0]], axis=2)
    blocks = to_blocks(whitened)
    twisted_blocks = to_blocks(twisted)
    norm_factor = 1.0 / jnp.sqrt(jnp.float32(WINDOWS * BAND))

    def cross(triple):
        mine, turned, other = triple
        mine32 = mine.astype(jnp.float32)
        turned32 = turned.astype(jnp.float32)
        other32 = other.astype(jnp.float32)
        real_sum = jnp.einsum('bik,bjk->bij', mine32, other32)
        imag_sum = jnp.einsum('bik,bjk->bij', turned32, other32)
        return jnp.concatenate([real_sum, imag_sum], axis=0) * norm_factor
    results = []
    for which_round in range(ROUNDS):
        others = jnp.roll(blocks, which_round + 1, axis=0)
        paired = lax.map(cross, (blocks, twisted_blocks, others))
        paired = jnp.transpose(paired, (1, 0, 2, 3)).reshape(2 * NB, CHANNELS, CH_DEV)
        results.append(paired)
    return jnp.stack(results)
```

```python
import functools
import math

import jax
import jax.numpy as jnp
import numpy as np
from jax import lax
from jax.experimental import pallas as pl
from jax.experimental.pallas import tpu as pltpu
from jax.sharding import PartitionSpec as P

NFFT = 2048
HALF = 1024
BAND = 64
SEG = 4096
WIN = 4
ROUNDS = 4
NB = 16
CH = 128
WINDOWS = 32
MESH = pl.DeviceIdType.MESH


def fourier_tables():
    position = np.arange(HALF, dtype=np.int64)[:, None]
    inner = np.arange(BAND // 2, dtype=np.int64)
    tables = []
    for parity in range(2):
        bins, imag = [], []
        for group in range(NB // 2):
            first, second = (group, group + 8) if parity == 0 else (group + 8, group)
            for is_imag in (False, True):
                for band in (first, second):
                    bins.append(band * BAND + 2 * inner + parity)
                    imag.append(np.full(inner.shape, is_imag))
        bins, imag = np.concatenate(bins)[None, :], np.concatenate(imag)[None, :]
        angle = (position * bins % NFFT).astype(np.float64) * (2.0 * math.pi / NFFT)
        tables.append(np.where(imag, -np.sin(angle), np.cos(angle)))
    table = np.stack(tables)
    high = table.astype(jnp.bfloat16)
    low = (table - high.astype(np.float64)).astype(jnp.bfloat16)
    return np.stack([high, low])


def kernel(
    traces, offsets, tables, out,
    ext, tab, turns, split, white, rec, acc, own_out, far_out, own_in, far_in,
    load_sem, tab_sem, halo_send, halo_recv, b_send, b_recv, c_send, c_recv, d_send, d_recv, known,
):
    chan, tm = lax.axis_index("chan"), lax.axis_index("tm")
    zl, x, core = chan // 8, chan // 2 % 4, chan % 2
    zh, y = tm // 4, tm % 4
    block = chan % 8
    band = 4 * x + y
    plane = zl * 8
    sibling = (chan + 1 - 2 * core, tm)
    following = jnp.where(core == 0, chan + 1, (zl + 1) % 4 * 8 + 2 * x)
    preceding = jnp.where(core == 0, (zl + 3) % 4 * 8 + 2 * x + 1, chan - 1)

    load = pltpu.make_async_copy(traces, ext.at[:, pl.ds(0, SEG)], load_sem)
    load.start()
    table_load = pltpu.make_async_copy(tables, tab, tab_sem)
    table_load.start()

    def x_peer(step):
        return (plane + (x + step) % 4 * 2 + core, tm)

    def y_peer(step):
        return (chan, zh * 4 + (y + step) % 4)

    partner = (chan, (1 - zh) * 4 + y)

    barrier = pltpu.get_barrier_semaphore()
    for step in range(1, 4):
        pl.semaphore_signal(barrier, inc=1, device_id=x_peer(step), device_id_type=MESH)
        pl.semaphore_signal(barrier, inc=1, device_id=y_peer(step), device_id_type=MESH)
    pl.semaphore_signal(barrier, inc=1, device_id=sibling, device_id_type=MESH)
    pl.semaphore_signal(barrier, inc=1, device_id=partner, device_id_type=MESH)
    pl.semaphore_signal(barrier, inc=1, device_id=(following, tm), device_id_type=MESH)
    pl.semaphore_signal(barrier, inc=1, device_id=(preceding, tm), device_id_type=MESH)

    @pl.when(tm == 4)
    def _():
        pl.semaphore_signal(barrier, inc=1, device_id=(chan, tm - 1), device_id_type=MESH)

    @pl.when(tm == 3)
    def _():
        pl.semaphore_signal(barrier, inc=1, device_id=(chan, tm + 1), device_id_type=MESH)

    at_fold = jnp.logical_or(tm == 3, tm == 4)

    @pl.when(at_fold)
    def _():
        pl.semaphore_wait(barrier, 11)

    @pl.when(jnp.logical_not(at_fold))
    def _():
        pl.semaphore_wait(barrier, 10)

    halo = pltpu.make_async_remote_copy(
        src_ref=traces.at[:, pl.ds(0, NFFT)],
        dst_ref=ext.at[:, pl.ds(SEG, NFFT)],
        send_sem=halo_send,
        recv_sem=halo_recv,
        device_id=(chan, jnp.maximum(tm - 1, 0)),
        device_id_type=MESH,
    )

    @pl.when(tm > 0)
    def _():
        halo.start()

    for step in range(1, 4):
        pl.semaphore_signal(known.at[0], inc=1, device_id=y_peer(step), device_id_type=MESH)
    pl.semaphore_wait(known.at[0], 3)
    pl.semaphore_signal(known.at[1], inc=1, device_id=sibling, device_id_type=MESH)
    pl.semaphore_wait(known.at[1], 1)
    pl.semaphore_signal(known.at[2], inc=1, device_id=partner, device_id_type=MESH)
    pl.semaphore_wait(known.at[2], 1)

    @pl.when(tm == 7)
    def _():
        ext[:, pl.ds(SEG, NFFT)] = jnp.zeros((CH, NFFT), jnp.float32)

    column = lax.broadcasted_iota(jnp.int32, (NB, 128), 1)
    row = lax.broadcasted_iota(jnp.int32, (NB, 128), 0)
    swapped = row // 8
    frequency = row * BAND + 2 * (column % 32) + (column // 32 + swapped) % 2
    for w in range(WIN):
        angle = (frequency * offsets[w] % NFFT).astype(jnp.float32) * (2.0 * math.pi / NFFT)
        turns[w, 0] = jnp.cos(angle)
        turns[w, 1] = jnp.where(column < 64, -1.0, 1.0) * jnp.sin(angle)

    load.wait()
    table_load.wait()

    @pl.when(tm < 7)
    def _():
        halo.wait_recv()

    lane = lax.broadcasted_iota(jnp.int32, (CH, 128), 1)
    even_quarter = lane // 32 % 2 == 0
    to_mine = block // 4 == core

    def b_copy(w, dx, dy):
        to_x, to_y = (x + dx) % 4, (y + dy) % 4
        return pltpu.make_async_remote_copy(
            src_ref=white.at[w, to_x * 4 + to_y],
            dst_ref=rec.at[w, y, 4 + block % 4],
            send_sem=b_send.at[w, dx * 4 + dy],
            recv_sem=b_recv.at[w, y, block % 4],
            device_id=(plane + to_x * 2 + block // 4, zh * 4 + to_y),
            device_id_type=MESH,
        )

    def transform(w, carry):
        start = offsets[w]
        parts = []
        for k in range(16):
            place = lane + 128 * k
            near, middle, far = (ext[:, pl.ds(NFFT * part + 128 * k, 128)] for part in range(3))
            parts.append(jnp.where(place >= start, near, jnp.where(place >= start - NFFT, middle, far)))
        mean = jnp.sum(functools.reduce(jnp.add, parts), axis=1, keepdims=True) * (1.0 / NFFT)
        parts = [part - mean for part in parts]
        power = jnp.sum(functools.reduce(jnp.add, [part * part for part in parts]), axis=1, keepdims=True)
        scale = lax.rsqrt(power * (1.0 / NFFT) + 1e-06)
        parts = [part * scale for part in parts]
        for k in range(8):
            for parity in range(2):
                value = parts[k] + parts[k + 8] if parity == 0 else parts[k] - parts[k + 8]
                high = value.astype(jnp.bfloat16)
                split[parity, pl.ds(0, CH), pl.ds(128 * k, 128)] = high
                split[parity, pl.ds(CH, CH), pl.ds(128 * k, 128)] = (value - high.astype(jnp.float32)).astype(jnp.bfloat16)
        for quarter in range(4):
            columns = pl.ds(256 * quarter, 256)
            both = []
            for parity in range(2):
                main = jnp.dot(split[parity], tab[0, parity, :, columns], preferred_element_type=jnp.float32)
                rest = jnp.dot(split[parity, pl.ds(0, CH), :], tab[1, parity, :, columns], preferred_element_type=jnp.float32)
                both.append(main[:CH] + main[CH:] + rest)
            for group in range(2):
                j = 2 * quarter + group
                even, odd = (part[:, 128 * group : 128 * group + 128] for part in both)
                for which, tile in ((j, jnp.where(even_quarter, even, odd)), (j + 8, jnp.where(even_quarter, odd, even))):
                    square = tile * tile
                    size = jnp.sqrt(square + pltpu.roll(square, 64, 1))
                    level = jnp.sum(size, axis=1, keepdims=True) * (0.5 / BAND)
                    tile = tile * (1.0 / (level + 1e-06))
                    straight = turns[w, 0, which : which + 1, :]
                    across = turns[w, 1, which : which + 1, :]
                    white[w, which] = (tile * straight + pltpu.roll(tile, 64, 1) * across).astype(jnp.bfloat16)
        for dx in range(4):
            for dy in range(4):
                if dx == 0 and dy == 0:

                    @pl.when(to_mine)
                    def _():
                        rec[w, y, 4 + block % 4] = white[w, band]

                    @pl.when(jnp.logical_not(to_mine))
                    def _():
                        b_copy(w, 0, 0).start()
                else:
                    b_copy(w, dx, dy).start()
        return carry

    lax.fori_loop(0, WIN, transform, 0)

    def c_copy(w, from_y):
        return pltpu.make_async_remote_copy(
            src_ref=rec.at[w, from_y, pl.ds(4, 4)],
            dst_ref=rec.at[w, from_y, pl.ds(0, 4)],
            send_sem=c_send.at[w, from_y],
            recv_sem=c_recv.at[w, from_y],
            device_id=(following, tm),
            device_id_type=MESH,
        )

    def forward(w):
        for from_y in range(4):
            for i in range(4):
                arrival = pltpu.make_async_remote_copy(
                    src_ref=white.at[w, 0],
                    dst_ref=rec.at[w, from_y, 4 + i],
                    send_sem=b_send.at[w, 0],
                    recv_sem=b_recv.at[w, from_y, i],
                    device_id=sibling,
                    device_id_type=MESH,
                )
                mine = jnp.logical_and(block == 4 * core + i, y == from_y)

                @pl.when(jnp.logical_not(mine))
                def _():
                    arrival.wait_recv()

            c_copy(w, from_y).start()

    sign = jnp.where(lane < 64, 1.0, -1.0)

    def cross(w, i):
        own = [rec[w, from_y, 4 + i] for from_y in range(4)]
        turned = [(pltpu.roll(tile.astype(jnp.float32), 64, 1) * sign).astype(jnp.bfloat16) for tile in own]
        left = jnp.concatenate([jnp.concatenate(own, axis=1), jnp.concatenate(turned, axis=1)], axis=0)
        right = jnp.concatenate([rec[w, from_y, pl.ds(i, 4)].reshape(4 * CH, 128) for from_y in range(4)], axis=1)
        return lax.dot_general(left, right, (((1,), (1,)), ((), ())), preferred_element_type=jnp.float32)

    def add_window(w):
        for from_y in range(4):
            c_copy(w, from_y).wait_recv()

        def one(i, carry):
            @pl.when(w == 0)
            def _():
                acc[i] = cross(w, i)

            @pl.when(w > 0)
            def _():
                acc[i] += cross(w, i)

            return carry

        lax.fori_loop(0, 4, one, 0)

    def exchange(w, carry):
        forward(w)

        @pl.when(w > 0)
        def _():
            add_window(w - 1)

        return carry

    lax.fori_loop(0, WIN, exchange, 0)
    for from_y in range(4):
        c_copy(WIN - 1, from_y).wait_recv()

    norm = 1.0 / math.sqrt(WINDOWS * BAND)

    def far_copy(i, dy):
        to_y = (y + dy) % 4
        return pltpu.make_async_remote_copy(
            src_ref=far_out.at[i, to_y],
            dst_ref=far_in.at[band],
            send_sem=d_send.at[0, i, dy],
            recv_sem=d_recv.at[0, band],
            device_id=(plane + 4 * core + i, (1 - zh) * 4 + to_y),
            device_id_type=MESH,
        )

    def own_copy(i, dy):
        to_y = (y + dy) % 4
        return pltpu.make_async_remote_copy(
            src_ref=own_out.at[i, to_y],
            dst_ref=own_in.at[band],
            send_sem=d_send.at[1, i, dy],
            recv_sem=d_recv.at[1, band],
            device_id=(plane + 4 * core + i, zh * 4 + to_y),
            device_id_type=MESH,
        )

    def give(step, carry):
        i = (step + x) % 4
        acc[i] = (acc[i] + cross(WIN - 1, i)) * norm
        for to_y in range(4):
            for r in range(ROUNDS):
                for part in range(2):
                    columns = pl.ds(128 * (ROUNDS - 1 - r), 128)
                    far_rows = pl.ds(pl.multiple_of(part * CH + 64 * (1 - zh) + 16 * to_y, 16), 16)
                    far_out[i, to_y, r, part] = acc[i, far_rows, columns].astype(jnp.bfloat16)
                    own_rows = pl.ds(pl.multiple_of(part * CH + 64 * zh + 16 * to_y, 16), 16)
                    own_out[i, to_y, r, part] = acc[i, own_rows, columns]
        for dy in range(4):
            far_copy(i, dy).start()
        for dy in range(4):
            if dy == 0:
                mine = block == 4 * core + i

                @pl.when(mine)
                def _():
                    own_in[band] = own_out[i, y]

                @pl.when(jnp.logical_not(mine))
                def _():
                    own_copy(i, 0).start()
            else:
                own_copy(i, dy).start()
        return carry

    lax.fori_loop(0, 4, give, 0)

    def take(m, carry):
        arrival = pltpu.make_async_remote_copy(
            src_ref=own_out.at[0, 0], dst_ref=own_in.at[m], send_sem=d_send.at[1, 0, 0],
            recv_sem=d_recv.at[1, m], device_id=sibling, device_id_type=MESH,
        )
        mine = jnp.logical_and(m == band, to_mine)

        @pl.when(jnp.logical_not(mine))
        def _():
            arrival.wait_recv()

        pltpu.make_async_remote_copy(
            src_ref=far_out.at[0, 0], dst_ref=far_in.at[m], send_sem=d_send.at[0, 0, 0],
            recv_sem=d_recv.at[0, m], device_id=sibling, device_id_type=MESH,
        ).wait_recv()
        for r in range(ROUNDS):
            for part in range(2):
                out[r, part * NB + m] = own_in[m, r, part] + far_in[m, r, part].astype(jnp.float32)
        return carry

    lax.fori_loop(0, NB, take, 0)

    @pl.when(tm > 0)
    def _():
        halo.wait_send()

    def b_left(w, carry):
        for dx in range(4):
            for dy in range(4):
                if dx == 0 and dy == 0:

                    @pl.when(jnp.logical_not(to_mine))
                    def _():
                        b_copy(w, 0, 0).wait_send()
                else:
                    b_copy(w, dx, dy).wait_send()
        for from_y in range(4):
            c_copy(w, from_y).wait_send()
        return carry

    lax.fori_loop(0, WIN, b_left, 0)

    def d_left(i, carry):
        for dy in range(4):
            far_copy(i, dy).wait_send()
            if dy == 0:

                @pl.when(block != 4 * core + i)
                def _():
                    own_copy(i, 0).wait_send()
            else:
                own_copy(i, dy).wait_send()
        return carry

    lax.fori_loop(0, 4, d_left, 0)


def per_device(traces, offsets):
    tables = jnp.asarray(fourier_tables())
    dma = pltpu.SemaphoreType.DMA
    piece = (ROUNDS, 2, 16, CH)
    return pl.pallas_call(
        kernel,
        out_shape=jax.ShapeDtypeStruct((ROUNDS, 2 * NB, 16, CH), jnp.float32),
        in_specs=[
            pl.BlockSpec(memory_space=pl.ANY),
            pl.BlockSpec(memory_space=pltpu.SMEM),
            pl.BlockSpec(memory_space=pl.ANY),
        ],
        out_specs=pl.BlockSpec(memory_space=pltpu.VMEM),
        scratch_shapes=[
            pltpu.VMEM((CH, SEG + NFFT), jnp.float32),
            pltpu.VMEM((2, 2, HALF, HALF), jnp.bfloat16),
            pltpu.VMEM((WIN, 2, NB, 128), jnp.float32),
            pltpu.VMEM((2, 2 * CH, HALF), jnp.bfloat16),
            pltpu.VMEM((WIN, NB, CH, 128), jnp.bfloat16),
            pltpu.VMEM((WIN, 4, 8, CH, 128), jnp.bfloat16),
            pltpu.VMEM((4, 2 * CH, ROUNDS * CH), jnp.float32),
            pltpu.VMEM((4, 4) + piece, jnp.float32),
            pltpu.VMEM((4, 4) + piece, jnp.bfloat16),
            pltpu.VMEM((NB,) + piece, jnp.float32),
            pltpu.VMEM((NB,) + piece, jnp.bfloat16),
            dma, dma, dma, dma,
            dma((WIN, 16)), dma((WIN, 4, 4)), dma((WIN, 4)), dma((WIN, 4)), dma((2, 4, 4)), dma((2, NB)),
            pltpu.SemaphoreType.REGULAR((3,)),
        ],
        compiler_params=pltpu.CompilerParams(
            collective_id=0, has_side_effects=True, vmem_limit_bytes=48 * 1024 * 1024
        ),
        cost_estimate=pl.CostEstimate(flops=8_000_000_000, bytes_accessed=16_000_000, transcendentals=1_000_000),
    )(traces, offsets, tables)


def solution(mesh):
    return jax.shard_map(
        per_device,
        mesh=mesh,
        in_specs=(P("chan", "tm"), P("tm")),
        out_specs=P(None, None, ("chan", "tm"), None),
        check_vma=False,
    )
```

```python
import functools
import math

import jax
import jax.numpy as jnp
import numpy as np
from jax import lax
from jax.experimental import pallas as pl
from jax.experimental.pallas import tpu as pltpu
from jax.sharding import PartitionSpec as P

NFFT = 2048
HALF = 1024
BAND = 64
SEG = 4096
WIN = 4
ROUNDS = 4
NB = 16
CH = 128
WINDOWS = 32
MESH = pl.DeviceIdType.MESH
FOLD = ((4, 7, 3), (4, 0, 3), (4, 5, 1, 3), (4, 6, 2, 3))
FAR_FIRST = (
    (2, 2), (2, 0), (0, 2), (2, 1), (3, 2), (2, 3), (1, 2), (1, 1), (3, 3), (1, 3), (3, 1), (1, 0), (3, 0), (0, 1), (0, 3),
)


def fourier_tables():
    position = np.arange(HALF, dtype=np.int64)[:, None]
    inner = np.arange(BAND // 2, dtype=np.int64)
    tables = []
    for parity in range(2):
        bins, imag = [], []
        for group in range(NB // 2):
            first, second = (group, group + 8) if parity == 0 else (group + 8, group)
            for is_imag in (False, True):
                for band in (first, second):
                    bins.append(band * BAND + 2 * inner + parity)
                    imag.append(np.full(inner.shape, is_imag))
        bins, imag = np.concatenate(bins)[None, :], np.concatenate(imag)[None, :]
        angle = (position * bins % NFFT).astype(np.float64) * (2.0 * math.pi / NFFT)
        tables.append(np.where(imag, -np.sin(angle), np.cos(angle)))
    table = np.stack(tables)
    high = table.astype(jnp.bfloat16)
    low = (table - high.astype(np.float64)).astype(jnp.bfloat16)
    return np.stack([high, low])


def kernel(
    traces, offsets, tables, out,
    ext, tab, turns, split, white, rec, acc, own_out, far_out, own_in, far_in,
    relay, load_sem, tab_sem, halo_send, halo_recv, fold_send, fold_recv, b_send, b_recv, c_send, c_recv, d_send, d_recv, known,
):
    chan, tm = lax.axis_index("chan"), lax.axis_index("tm")
    zl, x, core = chan // 8, chan // 2 % 4, chan % 2
    zh, y = tm // 4, tm % 4
    block = chan % 8
    band = 4 * x + y
    plane = zl * 8
    sibling = (chan + 1 - 2 * core, tm)
    following = jnp.where(core == 0, chan + 1, (zl + 1) % 4 * 8 + 2 * x)
    preceding = jnp.where(core == 0, (zl + 3) % 4 * 8 + 2 * x + 1, chan - 1)

    def x_peer(step):
        return (plane + (x + step) % 4 * 2 + core, tm)

    def y_peer(step):
        return (chan, zh * 4 + (y + step) % 4)

    partner = (chan, (1 - zh) * 4 + y)

    barrier = pltpu.get_barrier_semaphore()
    for step in range(1, 4):
        pl.semaphore_signal(barrier, inc=1, device_id=x_peer(step), device_id_type=MESH)
        pl.semaphore_signal(barrier, inc=1, device_id=y_peer(step), device_id_type=MESH)
    pl.semaphore_signal(barrier, inc=1, device_id=sibling, device_id_type=MESH)
    pl.semaphore_signal(barrier, inc=1, device_id=partner, device_id_type=MESH)
    pl.semaphore_signal(barrier, inc=1, device_id=(following, tm), device_id_type=MESH)
    pl.semaphore_signal(barrier, inc=1, device_id=(preceding, tm), device_id_type=MESH)

    pl.semaphore_wait(barrier, 10)

    halo = pltpu.make_async_remote_copy(
        src_ref=traces.at[:, pl.ds(0, NFFT)],
        dst_ref=ext.at[:, pl.ds(SEG, NFFT)],
        send_sem=halo_send,
        recv_sem=halo_recv,
        device_id=(chan, jnp.maximum(tm - 1, 0)),
        device_id_type=MESH,
    )
    direct_out = jnp.logical_and(tm > 0, tm != 4)
    direct_in = jnp.logical_and(tm < 7, tm != 3)

    def fold_copy(way, piece, leg):
        first, last = leg == 0, leg == len(FOLD[way]) - 2
        rows = pl.ds(32 * way + 8 * piece, 8)
        return pltpu.make_async_remote_copy(
            src_ref=traces.at[rows, pl.ds(0, NFFT)] if first else relay.at[piece],
            dst_ref=ext.at[rows, pl.ds(SEG, NFFT)] if last else relay.at[piece],
            send_sem=fold_send.at[way, piece],
            recv_sem=fold_recv.at[way, piece],
            device_id=(chan, jnp.int32(FOLD[way][leg + 1])),
            device_id_type=MESH,
        )

    @pl.when(direct_out)
    def _():
        halo.start()

    @pl.when(tm == 4)
    def _():
        for piece in range(4):
            for way in range(4):
                fold_copy(way, piece, 0).start()

    load = pltpu.make_async_copy(traces, ext.at[:, pl.ds(0, SEG)], load_sem)
    load.start()
    table_load = pltpu.make_async_copy(tables, tab, tab_sem)
    table_load.start()

    for step in range(1, 4):
        pl.semaphore_signal(known.at[0], inc=1, device_id=y_peer(step), device_id_type=MESH)
    pl.semaphore_wait(known.at[0], 3)
    pl.semaphore_signal(known.at[1], inc=1, device_id=sibling, device_id_type=MESH)
    pl.semaphore_wait(known.at[1], 1)
    pl.semaphore_signal(known.at[2], inc=1, device_id=partner, device_id_type=MESH)
    pl.semaphore_wait(known.at[2], 1)

    @pl.when(tm == 7)
    def _():
        ext[:, pl.ds(SEG, NFFT)] = jnp.zeros((CH, NFFT), jnp.float32)

    column = lax.broadcasted_iota(jnp.int32, (NB, 128), 1)
    row = lax.broadcasted_iota(jnp.int32, (NB, 128), 0)
    swapped = row // 8
    frequency = row * BAND + 2 * (column % 32) + (column // 32 + swapped) % 2
    for w in range(WIN):
        angle = (frequency * offsets[w] % NFFT).astype(jnp.float32) * (2.0 * math.pi / NFFT)
        turns[w, 0] = jnp.cos(angle)
        turns[w, 1] = jnp.where(column < 64, -1.0, 1.0) * jnp.sin(angle)

    load.wait()
    table_load.wait()

    for way, path in enumerate(FOLD):
        for leg in range(1, len(path) - 1):

            @pl.when(tm == path[leg])
            def _():
                for piece in range(4):
                    fold_copy(way, piece, leg - 1).wait_recv()
                    fold_copy(way, piece, leg).start()

    @pl.when(direct_in)
    def _():
        halo.wait_recv()

    @pl.when(tm == 3)
    def _():
        for way, path in enumerate(FOLD):
            for piece in range(4):
                fold_copy(way, piece, len(path) - 2).wait_recv()

    for step in range(1, 4):
        pl.semaphore_signal(known.at[3], inc=1, device_id=y_peer(step), device_id_type=MESH)
    pl.semaphore_wait(known.at[3], 3)

    lane = lax.broadcasted_iota(jnp.int32, (CH, 128), 1)
    even_quarter = lane // 32 % 2 == 0
    to_mine = block // 4 == core

    def b_copy(w, dx, dy):
        to_x, to_y = (x + dx) % 4, (y + dy) % 4
        return pltpu.make_async_remote_copy(
            src_ref=white.at[w, to_x * 4 + to_y],
            dst_ref=rec.at[w, y, 4 + block % 4],
            send_sem=b_send.at[w, dx * 4 + dy],
            recv_sem=b_recv.at[w, y, block % 4],
            device_id=(plane + to_x * 2 + block // 4, zh * 4 + to_y),
            device_id_type=MESH,
        )

    def transform(w, carry):
        start = offsets[w]
        parts = []
        for k in range(16):
            place = lane + 128 * k
            near, middle, far = (ext[:, pl.ds(NFFT * part + 128 * k, 128)] for part in range(3))
            parts.append(jnp.where(place >= start, near, jnp.where(place >= start - NFFT, middle, far)))
        mean = jnp.sum(functools.reduce(jnp.add, parts), axis=1, keepdims=True) * (1.0 / NFFT)
        parts = [part - mean for part in parts]
        power = jnp.sum(functools.reduce(jnp.add, [part * part for part in parts]), axis=1, keepdims=True)
        scale = lax.rsqrt(power * (1.0 / NFFT) + 1e-06)
        parts = [part * scale for part in parts]
        for k in range(8):
            for parity in range(2):
                value = parts[k] + parts[k + 8] if parity == 0 else parts[k] - parts[k + 8]
                high = value.astype(jnp.bfloat16)
                split[parity, pl.ds(0, CH), pl.ds(128 * k, 128)] = high
                split[parity, pl.ds(CH, CH), pl.ds(128 * k, 128)] = (value - high.astype(jnp.float32)).astype(jnp.bfloat16)
        for quarter in range(4):
            columns = pl.ds(256 * quarter, 256)
            both = []
            for parity in range(2):
                main = jnp.dot(split[parity], tab[0, parity, :, columns], preferred_element_type=jnp.float32)
                rest = jnp.dot(split[parity, pl.ds(0, CH), :], tab[1, parity, :, columns], preferred_element_type=jnp.float32)
                both.append(main[:CH] + main[CH:] + rest)
            for group in range(2):
                j = 2 * quarter + group
                even, odd = (part[:, 128 * group : 128 * group + 128] for part in both)
                for which, tile in ((j, jnp.where(even_quarter, even, odd)), (j + 8, jnp.where(even_quarter, odd, even))):
                    square = tile * tile
                    size = jnp.sqrt(square + pltpu.roll(square, 64, 1))
                    level = jnp.sum(size, axis=1, keepdims=True) * (0.5 / BAND)
                    tile = tile * (1.0 / (level + 1e-06))
                    straight = turns[w, 0, which : which + 1, :]
                    across = turns[w, 1, which : which + 1, :]
                    white[w, which] = (tile * straight + pltpu.roll(tile, 64, 1) * across).astype(jnp.bfloat16)
        for dx, dy in FAR_FIRST:
            b_copy(w, dx, dy).start()

        @pl.when(to_mine)
        def _():
            rec[w, y, 4 + block % 4] = white[w, band]

        @pl.when(jnp.logical_not(to_mine))
        def _():
            b_copy(w, 0, 0).start()

        return carry

    lax.fori_loop(0, WIN, transform, 0)

    def c_copy(w, from_y):
        return pltpu.make_async_remote_copy(
            src_ref=rec.at[w, from_y, pl.ds(4, 4)],
            dst_ref=rec.at[w, from_y, pl.ds(0, 4)],
            send_sem=c_send.at[w, from_y],
            recv_sem=c_recv.at[w, from_y],
            device_id=(following, tm),
            device_id_type=MESH,
        )

    def forward(w):
        for from_y in range(4):
            for i in range(4):
                arrival = pltpu.make_async_remote_copy(
                    src_ref=white.at[w, 0],
                    dst_ref=rec.at[w, from_y, 4 + i],
                    send_sem=b_send.at[w, 0],
                    recv_sem=b_recv.at[w, from_y, i],
                    device_id=sibling,
                    device_id_type=MESH,
                )
                mine = jnp.logical_and(block == 4 * core + i, y == from_y)

                @pl.when(jnp.logical_not(mine))
                def _():
                    arrival.wait_recv()

            c_copy(w, from_y).start()

    sign = jnp.where(lane < 64, 1.0, -1.0)

    def cross(w, i):
        own = [rec[w, from_y, 4 + i] for from_y in range(4)]
        turned = [(pltpu.roll(tile.astype(jnp.float32), 64, 1) * sign).astype(jnp.bfloat16) for tile in own]
        left = jnp.concatenate([jnp.concatenate(own, axis=1), jnp.concatenate(turned, axis=1)], axis=0)
        right = jnp.concatenate([rec[w, from_y, pl.ds(i, 4)].reshape(4 * CH, 128) for from_y in range(4)], axis=1)
        return lax.dot_general(left, right, (((1,), (1,)), ((), ())), preferred_element_type=jnp.float32)

    def add_window(w):
        for from_y in range(4):
            c_copy(w, from_y).wait_recv()

        def one(i, carry):
            @pl.when(w == 0)
            def _():
                acc[i] = cross(w, i)

            @pl.when(w > 0)
            def _():
                acc[i] += cross(w, i)

            return carry

        lax.fori_loop(0, 4, one, 0)

    def exchange(w, carry):
        forward(w)

        @pl.when(w > 0)
        def _():
            add_window(w - 1)

        return carry

    lax.fori_loop(0, WIN, exchange, 0)
    for from_y in range(4):
        c_copy(WIN - 1, from_y).wait_recv()

    norm = 1.0 / math.sqrt(WINDOWS * BAND)

    def far_copy(i, dy):
        to_y = (y + dy) % 4
        return pltpu.make_async_remote_copy(
            src_ref=far_out.at[i, to_y],
            dst_ref=far_in.at[band],
            send_sem=d_send.at[0, i, dy],
            recv_sem=d_recv.at[0, band],
            device_id=(plane + 4 * core + i, (1 - zh) * 4 + to_y),
            device_id_type=MESH,
        )

    def own_copy(i, dy):
        to_y = (y + dy) % 4
        return pltpu.make_async_remote_copy(
            src_ref=own_out.at[i, to_y],
            dst_ref=own_in.at[band],
            send_sem=d_send.at[1, i, dy],
            recv_sem=d_recv.at[1, band],
            device_id=(plane + 4 * core + i, zh * 4 + to_y),
            device_id_type=MESH,
        )

    def give(step, carry):
        i = (step + x) % 4
        acc[i] = (acc[i] + cross(WIN - 1, i)) * norm
        for to_y in range(4):
            for r in range(ROUNDS):
                for part in range(2):
                    columns = pl.ds(128 * (ROUNDS - 1 - r), 128)
                    far_rows = pl.ds(pl.multiple_of(part * CH + 64 * (1 - zh) + 16 * to_y, 16), 16)
                    far_out[i, to_y, r, part] = acc[i, far_rows, columns].astype(jnp.bfloat16)
                    own_rows = pl.ds(pl.multiple_of(part * CH + 64 * zh + 16 * to_y, 16), 16)
                    own_out[i, to_y, r, part] = acc[i, own_rows, columns]
        for dy in range(4):
            far_copy(i, dy).start()
        for dy in range(4):
            if dy == 0:
                mine = block == 4 * core + i

                @pl.when(mine)
                def _():
                    own_in[band] = own_out[i, y]

                @pl.when(jnp.logical_not(mine))
                def _():
                    own_copy(i, 0).start()
            else:
                own_copy(i, dy).start()
        return carry

    lax.fori_loop(0, 4, give, 0)

    def take(m, carry):
        arrival = pltpu.make_async_remote_copy(
            src_ref=own_out.at[0, 0], dst_ref=own_in.at[m], send_sem=d_send.at[1, 0, 0],
            recv_sem=d_recv.at[1, m], device_id=sibling, device_id_type=MESH,
        )
        mine = jnp.logical_and(m == band, to_mine)

        @pl.when(jnp.logical_not(mine))
        def _():
            arrival.wait_recv()

        pltpu.make_async_remote_copy(
            src_ref=far_out.at[0, 0], dst_ref=far_in.at[m], send_sem=d_send.at[0, 0, 0],
            recv_sem=d_recv.at[0, m], device_id=sibling, device_id_type=MESH,
        ).wait_recv()
        for r in range(ROUNDS):
            for part in range(2):
                out[r, part * NB + m] = own_in[m, r, part] + far_in[m, r, part].astype(jnp.float32)
        return carry

    lax.fori_loop(0, NB, take, 0)

    @pl.when(direct_out)
    def _():
        halo.wait_send()

    for way, path in enumerate(FOLD):
        for leg in range(len(path) - 1):

            @pl.when(tm == path[leg])
            def _():
                for piece in range(4):
                    fold_copy(way, piece, leg).wait_send()

    def b_left(w, carry):
        for dx in range(4):
            for dy in range(4):
                if dx == 0 and dy == 0:

                    @pl.when(jnp.logical_not(to_mine))
                    def _():
                        b_copy(w, 0, 0).wait_send()
                else:
                    b_copy(w, dx, dy).wait_send()
        for from_y in range(4):
            c_copy(w, from_y).wait_send()
        return carry

    lax.fori_loop(0, WIN, b_left, 0)

    def d_left(i, carry):
        for dy in range(4):
            far_copy(i, dy).wait_send()
            if dy == 0:

                @pl.when(block != 4 * core + i)
                def _():
                    own_copy(i, 0).wait_send()
            else:
                own_copy(i, dy).wait_send()
        return carry

    lax.fori_loop(0, 4, d_left, 0)


def per_device(traces, offsets):
    tables = jnp.asarray(fourier_tables())
    dma = pltpu.SemaphoreType.DMA
    piece = (ROUNDS, 2, 16, CH)
    return pl.pallas_call(
        kernel,
        out_shape=jax.ShapeDtypeStruct((ROUNDS, 2 * NB, 16, CH), jnp.float32),
        in_specs=[
            pl.BlockSpec(memory_space=pl.ANY),
            pl.BlockSpec(memory_space=pltpu.SMEM),
            pl.BlockSpec(memory_space=pl.ANY),
        ],
        out_specs=pl.BlockSpec(memory_space=pltpu.VMEM),
        scratch_shapes=[
            pltpu.VMEM((CH, SEG + NFFT), jnp.float32),
            pltpu.VMEM((2, 2, HALF, HALF), jnp.bfloat16),
            pltpu.VMEM((WIN, 2, NB, 128), jnp.float32),
            pltpu.VMEM((2, 2 * CH, HALF), jnp.bfloat16),
            pltpu.VMEM((WIN, NB, CH, 128), jnp.bfloat16),
            pltpu.VMEM((WIN, 4, 8, CH, 128), jnp.bfloat16),
            pltpu.VMEM((4, 2 * CH, ROUNDS * CH), jnp.float32),
            pltpu.VMEM((4, 4) + piece, jnp.float32),
            pltpu.VMEM((4, 4) + piece, jnp.bfloat16),
            pltpu.VMEM((NB,) + piece, jnp.float32),
            pltpu.VMEM((NB,) + piece, jnp.bfloat16),
            pltpu.VMEM((4, 8, NFFT), jnp.float32),
            dma, dma, dma, dma, dma((4, 4)), dma((4, 4)),
            dma((WIN, 16)), dma((WIN, 4, 4)), dma((WIN, 4)), dma((WIN, 4)), dma((2, 4, 4)), dma((2, NB)),
            pltpu.SemaphoreType.REGULAR((4,)),
        ],
        compiler_params=pltpu.CompilerParams(
            collective_id=0, has_side_effects=True, vmem_limit_bytes=60 * 1024 * 1024
        ),
        cost_estimate=pl.CostEstimate(flops=8_000_000_000, bytes_accessed=16_000_000, transcendentals=1_000_000),
    )(traces, offsets, tables)


def solution(mesh):
    return jax.shard_map(
        per_device,
        mesh=mesh,
        in_specs=(P("chan", "tm"), P("tm")),
        out_specs=P(None, None, ("chan", "tm"), None),
        check_vma=False,
    )
```

```python
import functools
import math

import jax
import jax.numpy as jnp
import numpy as np
from jax import lax
from jax.experimental import pallas as pl
from jax.experimental.pallas import tpu as pltpu
from jax.sharding import PartitionSpec as P

NFFT = 2048
HALF = 1024
BAND = 64
SEG = 4096
WIN = 4
ROUNDS = 4
NB = 16
CH = 128
WINDOWS = 32
MESH = pl.DeviceIdType.MESH
FOLD = (((4, 7, 3), range(0, 6)), ((4, 0, 3), range(6, 12)), ((4, 5, 1, 2, 3), range(12, 16)))
FOLD_ORDER = (12, 0, 6, 13, 1, 7, 14, 2, 8, 15, 3, 9, 4, 10, 5, 11)
FAR_FIRST = (
    (2, 2), (2, 0), (0, 2), (2, 1), (3, 2), (2, 3), (1, 2), (1, 1), (3, 3), (1, 3), (3, 1), (1, 0), (3, 0), (0, 1), (0, 3),
)


def fourier_tables():
    position = np.arange(HALF, dtype=np.int64)[:, None]
    inner = np.arange(BAND // 2, dtype=np.int64)
    tables = []
    for parity in range(2):
        bins, imag = [], []
        for group in range(NB // 2):
            first, second = (group, group + 8) if parity == 0 else (group + 8, group)
            for is_imag in (False, True):
                for band in (first, second):
                    bins.append(band * BAND + 2 * inner + parity)
                    imag.append(np.full(inner.shape, is_imag))
        bins, imag = np.concatenate(bins)[None, :], np.concatenate(imag)[None, :]
        angle = (position * bins % NFFT).astype(np.float64) * (2.0 * math.pi / NFFT)
        tables.append(np.where(imag, -np.sin(angle), np.cos(angle)))
    table = np.stack(tables)
    high = table.astype(jnp.bfloat16)
    low = (table - high.astype(np.float64)).astype(jnp.bfloat16)
    return np.stack([high, low])


def kernel(
    traces, offsets, tables, out,
    ext, tab, turns, split, white, rec, acc, own_out, far_out, own_in, far_in,
    relay, load_sem, tab_sem, halo_send, halo_recv, fold_send, fold_recv, b_send, b_recv, c_send, c_recv, d_send, d_recv, known,
):
    chan, tm = lax.axis_index("chan"), lax.axis_index("tm")
    zl, x, core = chan // 8, chan // 2 % 4, chan % 2
    zh, y = tm // 4, tm % 4
    block = chan % 8
    band = 4 * x + y
    plane = zl * 8
    sibling = (chan + 1 - 2 * core, tm)
    following = jnp.where(core == 0, chan + 1, (zl + 1) % 4 * 8 + 2 * x)
    preceding = jnp.where(core == 0, (zl + 3) % 4 * 8 + 2 * x + 1, chan - 1)

    def x_peer(step):
        return (plane + (x + step) % 4 * 2 + core, tm)

    def y_peer(step):
        return (chan, zh * 4 + (y + step) % 4)

    partner = (chan, (1 - zh) * 4 + y)

    barrier = pltpu.get_barrier_semaphore()
    for step in range(1, 4):
        pl.semaphore_signal(barrier, inc=1, device_id=x_peer(step), device_id_type=MESH)
        pl.semaphore_signal(barrier, inc=1, device_id=y_peer(step), device_id_type=MESH)
    pl.semaphore_signal(barrier, inc=1, device_id=sibling, device_id_type=MESH)
    pl.semaphore_signal(barrier, inc=1, device_id=partner, device_id_type=MESH)
    pl.semaphore_signal(barrier, inc=1, device_id=(following, tm), device_id_type=MESH)
    pl.semaphore_signal(barrier, inc=1, device_id=(preceding, tm), device_id_type=MESH)

    pl.semaphore_wait(barrier, 10)

    halo = pltpu.make_async_remote_copy(
        src_ref=traces.at[:, pl.ds(0, NFFT)],
        dst_ref=ext.at[:, pl.ds(SEG, NFFT)],
        send_sem=halo_send,
        recv_sem=halo_recv,
        device_id=(chan, jnp.maximum(tm - 1, 0)),
        device_id_type=MESH,
    )
    direct_out = jnp.logical_and(tm > 0, tm != 4)
    direct_in = jnp.logical_and(tm < 7, tm != 3)

    def fold_copy(path, piece, leg):
        first, last = leg == 0, leg == len(path) - 2
        rows = pl.ds(8 * piece, 8)
        return pltpu.make_async_remote_copy(
            src_ref=traces.at[rows, pl.ds(0, NFFT)] if first else relay.at[piece],
            dst_ref=ext.at[rows, pl.ds(SEG, NFFT)] if last else relay.at[piece],
            send_sem=fold_send.at[piece],
            recv_sem=fold_recv.at[piece],
            device_id=(chan, jnp.int32(path[leg + 1])),
            device_id_type=MESH,
        )

    @pl.when(direct_out)
    def _():
        halo.start()

    @pl.when(tm == 4)
    def _():
        for piece in FOLD_ORDER:
            path = next(path for path, pieces in FOLD if piece in pieces)
            fold_copy(path, piece, 0).start()

    load = pltpu.make_async_copy(traces, ext.at[:, pl.ds(0, SEG)], load_sem)
    load.start()
    table_load = pltpu.make_async_copy(tables, tab, tab_sem)
    table_load.start()

    for step in range(1, 4):
        pl.semaphore_signal(known.at[0], inc=1, device_id=y_peer(step), device_id_type=MESH)
    pl.semaphore_wait(known.at[0], 3)
    pl.semaphore_signal(known.at[1], inc=1, device_id=sibling, device_id_type=MESH)
    pl.semaphore_wait(known.at[1], 1)
    pl.semaphore_signal(known.at[2], inc=1, device_id=partner, device_id_type=MESH)
    pl.semaphore_wait(known.at[2], 1)

    @pl.when(tm == 7)
    def _():
        ext[:, pl.ds(SEG, NFFT)] = jnp.zeros((CH, NFFT), jnp.float32)

    column = lax.broadcasted_iota(jnp.int32, (NB, 128), 1)
    row = lax.broadcasted_iota(jnp.int32, (NB, 128), 0)
    swapped = row // 8
    frequency = row * BAND + 2 * (column % 32) + (column // 32 + swapped) % 2
    for w in range(WIN):
        angle = (frequency * offsets[w] % NFFT).astype(jnp.float32) * (2.0 * math.pi / NFFT)
        turns[w, 0] = jnp.cos(angle)
        turns[w, 1] = jnp.where(column < 64, -1.0, 1.0) * jnp.sin(angle)

    load.wait()
    table_load.wait()

    for path, pieces in FOLD:
        for leg in range(1, len(path) - 1):

            @pl.when(tm == path[leg])
            def _():
                for piece in pieces:
                    fold_copy(path, piece, leg - 1).wait_recv()
                    fold_copy(path, piece, leg).start()

    @pl.when(direct_in)
    def _():
        halo.wait_recv()

    @pl.when(tm == 3)
    def _():
        for path, pieces in FOLD:
            for piece in pieces:
                fold_copy(path, piece, len(path) - 2).wait_recv()

    for step in range(1, 4):
        pl.semaphore_signal(known.at[3], inc=1, device_id=y_peer(step), device_id_type=MESH)
    pl.semaphore_wait(known.at[3], 3)

    lane = lax.broadcasted_iota(jnp.int32, (CH, 128), 1)
    even_quarter = lane // 32 % 2 == 0
    to_mine = block // 4 == core

    def b_copy(w, dx, dy):
        to_x, to_y = (x + dx) % 4, (y + dy) % 4
        return pltpu.make_async_remote_copy(
            src_ref=white.at[w, to_x * 4 + to_y],
            dst_ref=rec.at[w, y, 4 + block % 4],
            send_sem=b_send.at[w, dx * 4 + dy],
            recv_sem=b_recv.at[w, y, block % 4],
            device_id=(plane + to_x * 2 + block // 4, zh * 4 + to_y),
            device_id_type=MESH,
        )

    def transform(w, carry):
        start = offsets[w]
        parts = []
        for k in range(16):
            place = lane + 128 * k
            near, middle, far = (ext[:, pl.ds(NFFT * part + 128 * k, 128)] for part in range(3))
            parts.append(jnp.where(place >= start, near, jnp.where(place >= start - NFFT, middle, far)))
        mean = jnp.sum(functools.reduce(jnp.add, parts), axis=1, keepdims=True) * (1.0 / NFFT)
        parts = [part - mean for part in parts]
        power = jnp.sum(functools.reduce(jnp.add, [part * part for part in parts]), axis=1, keepdims=True)
        scale = lax.rsqrt(power * (1.0 / NFFT) + 1e-06)
        parts = [part * scale for part in parts]
        for k in range(8):
            for parity in range(2):
                value = parts[k] + parts[k + 8] if parity == 0 else parts[k] - parts[k + 8]
                high = value.astype(jnp.bfloat16)
                split[parity, pl.ds(0, CH), pl.ds(128 * k, 128)] = high
                split[parity, pl.ds(CH, CH), pl.ds(128 * k, 128)] = (value - high.astype(jnp.float32)).astype(jnp.bfloat16)
        for quarter in range(4):
            columns = pl.ds(256 * quarter, 256)
            both = []
            for parity in range(2):
                main = jnp.dot(split[parity], tab[0, parity, :, columns], preferred_element_type=jnp.float32)
                rest = jnp.dot(split[parity, pl.ds(0, CH), :], tab[1, parity, :, columns], preferred_element_type=jnp.float32)
                both.append(main[:CH] + main[CH:] + rest)
            for group in range(2):
                j = 2 * quarter + group
                even, odd = (part[:, 128 * group : 128 * group + 128] for part in both)
                for which, tile in ((j, jnp.where(even_quarter, even, odd)), (j + 8, jnp.where(even_quarter, odd, even))):
                    square = tile * tile
                    size = jnp.sqrt(square + pltpu.roll(square, 64, 1))
                    level = jnp.sum(size, axis=1, keepdims=True) * (0.5 / BAND)
                    tile = tile * (1.0 / (level + 1e-06))
                    straight = turns[w, 0, which : which + 1, :]
                    across = turns[w, 1, which : which + 1, :]
                    white[w, which] = (tile * straight + pltpu.roll(tile, 64, 1) * across).astype(jnp.bfloat16)
        for dx, dy in FAR_FIRST:
            b_copy(w, dx, dy).start()

        @pl.when(to_mine)
        def _():
            rec[w, y, 4 + block % 4] = white[w, band]

        @pl.when(jnp.logical_not(to_mine))
        def _():
            b_copy(w, 0, 0).start()

        return carry

    lax.fori_loop(0, WIN, transform, 0)

    def c_copy(w, from_y, i):
        return pltpu.make_async_remote_copy(
            src_ref=rec.at[w, from_y, 4 + i],
            dst_ref=rec.at[w, from_y, i],
            send_sem=c_send.at[w, from_y, i],
            recv_sem=c_recv.at[w, from_y, i],
            device_id=(following, tm),
            device_id_type=MESH,
        )

    def forward(w):
        for turn in (2, 3, 1, 0):
            from_y = (y + turn) % 4
            for i in range(4):
                arrival = pltpu.make_async_remote_copy(
                    src_ref=white.at[w, 0],
                    dst_ref=rec.at[w, from_y, 4 + i],
                    send_sem=b_send.at[w, 0],
                    recv_sem=b_recv.at[w, from_y, i],
                    device_id=sibling,
                    device_id_type=MESH,
                )
                mine = jnp.logical_and(block == 4 * core + i, y == from_y)

                @pl.when(jnp.logical_not(mine))
                def _():
                    arrival.wait_recv()

                c_copy(w, from_y, i).start()

    sign = jnp.where(lane < 64, 1.0, -1.0)

    def cross(w, i):
        own = [rec[w, from_y, 4 + i] for from_y in range(4)]
        turned = [(pltpu.roll(tile.astype(jnp.float32), 64, 1) * sign).astype(jnp.bfloat16) for tile in own]
        left = jnp.concatenate([jnp.concatenate(own, axis=1), jnp.concatenate(turned, axis=1)], axis=0)
        right = jnp.concatenate([rec[w, from_y, pl.ds(i, 4)].reshape(4 * CH, 128) for from_y in range(4)], axis=1)
        return lax.dot_general(left, right, (((1,), (1,)), ((), ())), preferred_element_type=jnp.float32)

    def add_window(w):
        for from_y in range(4):
            for i in range(4):
                c_copy(w, from_y, i).wait_recv()

        def one(i, carry):
            @pl.when(w == 0)
            def _():
                acc[i] = cross(w, i)

            @pl.when(w > 0)
            def _():
                acc[i] += cross(w, i)

            return carry

        lax.fori_loop(0, 4, one, 0)

    def exchange(w, carry):
        forward(w)

        @pl.when(w > 0)
        def _():
            add_window(w - 1)

        return carry

    lax.fori_loop(0, WIN, exchange, 0)
    for from_y in range(4):
        for i in range(4):
            c_copy(WIN - 1, from_y, i).wait_recv()

    norm = 1.0 / math.sqrt(WINDOWS * BAND)

    def far_copy(i, dy):
        to_y = (y + dy) % 4
        return pltpu.make_async_remote_copy(
            src_ref=far_out.at[i, to_y],
            dst_ref=far_in.at[band],
            send_sem=d_send.at[0, i, dy],
            recv_sem=d_recv.at[0, band],
            device_id=(plane + 4 * core + i, (1 - zh) * 4 + to_y),
            device_id_type=MESH,
        )

    def own_copy(i, dy):
        to_y = (y + dy) % 4
        return pltpu.make_async_remote_copy(
            src_ref=own_out.at[i, to_y],
            dst_ref=own_in.at[band],
            send_sem=d_send.at[1, i, dy],
            recv_sem=d_recv.at[1, band],
            device_id=(plane + 4 * core + i, zh * 4 + to_y),
            device_id_type=MESH,
        )

    def give(step, carry):
        i = (step + x) % 4
        acc[i] = (acc[i] + cross(WIN - 1, i)) * norm
        for to_y in range(4):
            for r in range(ROUNDS):
                for part in range(2):
                    columns = pl.ds(128 * (ROUNDS - 1 - r), 128)
                    far_rows = pl.ds(pl.multiple_of(part * CH + 64 * (1 - zh) + 16 * to_y, 16), 16)
                    far_out[i, to_y, r, part] = acc[i, far_rows, columns].astype(jnp.bfloat16)
                    own_rows = pl.ds(pl.multiple_of(part * CH + 64 * zh + 16 * to_y, 16), 16)
                    own_out[i, to_y, r, part] = acc[i, own_rows, columns]
        for dy in range(4):
            far_copy(i, dy).start()
        for dy in range(4):
            if dy == 0:
                mine = block == 4 * core + i

                @pl.when(mine)
                def _():
                    own_in[band] = own_out[i, y]

                @pl.when(jnp.logical_not(mine))
                def _():
                    own_copy(i, 0).start()
            else:
                own_copy(i, dy).start()
        return carry

    for step in range(1, 4):
        pl.semaphore_signal(known.at[4], inc=1, device_id=y_peer(step), device_id_type=MESH)
        pl.semaphore_signal(known.at[4], inc=1, device_id=x_peer(step), device_id_type=MESH)
    pl.semaphore_signal(known.at[4], inc=1, device_id=partner, device_id_type=MESH)
    pl.semaphore_signal(known.at[4], inc=1, device_id=sibling, device_id_type=MESH)
    pl.semaphore_wait(known.at[4], 8)
    lax.fori_loop(0, 4, give, 0)

    def take(m, carry):
        arrival = pltpu.make_async_remote_copy(
            src_ref=own_out.at[0, 0], dst_ref=own_in.at[m], send_sem=d_send.at[1, 0, 0],
            recv_sem=d_recv.at[1, m], device_id=sibling, device_id_type=MESH,
        )
        mine = jnp.logical_and(m == band, to_mine)

        @pl.when(jnp.logical_not(mine))
        def _():
            arrival.wait_recv()

        pltpu.make_async_remote_copy(
            src_ref=far_out.at[0, 0], dst_ref=far_in.at[m], send_sem=d_send.at[0, 0, 0],
            recv_sem=d_recv.at[0, m], device_id=sibling, device_id_type=MESH,
        ).wait_recv()
        for r in range(ROUNDS):
            for part in range(2):
                out[r, part * NB + m] = own_in[m, r, part] + far_in[m, r, part].astype(jnp.float32)
        return carry

    lax.fori_loop(0, NB, take, 0)

    @pl.when(direct_out)
    def _():
        halo.wait_send()

    for path, pieces in FOLD:
        for leg in range(len(path) - 1):

            @pl.when(tm == path[leg])
            def _():
                for piece in pieces:
                    fold_copy(path, piece, leg).wait_send()

    def b_left(w, carry):
        for dx in range(4):
            for dy in range(4):
                if dx == 0 and dy == 0:

                    @pl.when(jnp.logical_not(to_mine))
                    def _():
                        b_copy(w, 0, 0).wait_send()
                else:
                    b_copy(w, dx, dy).wait_send()
        for from_y in range(4):
            for i in range(4):
                c_copy(w, from_y, i).wait_send()
        return carry

    lax.fori_loop(0, WIN, b_left, 0)

    def d_left(i, carry):
        for dy in range(4):
            far_copy(i, dy).wait_send()
            if dy == 0:

                @pl.when(block != 4 * core + i)
                def _():
                    own_copy(i, 0).wait_send()
            else:
                own_copy(i, dy).wait_send()
        return carry

    lax.fori_loop(0, 4, d_left, 0)


def per_device(traces, offsets):
    tables = jnp.asarray(fourier_tables())
    dma = pltpu.SemaphoreType.DMA
    piece = (ROUNDS, 2, 16, CH)
    return pl.pallas_call(
        kernel,
        out_shape=jax.ShapeDtypeStruct((ROUNDS, 2 * NB, 16, CH), jnp.float32),
        in_specs=[
            pl.BlockSpec(memory_space=pl.ANY),
            pl.BlockSpec(memory_space=pltpu.SMEM),
            pl.BlockSpec(memory_space=pl.ANY),
        ],
        out_specs=pl.BlockSpec(memory_space=pltpu.VMEM),
        scratch_shapes=[
            pltpu.VMEM((CH, SEG + NFFT), jnp.float32),
            pltpu.VMEM((2, 2, HALF, HALF), jnp.bfloat16),
            pltpu.VMEM((WIN, 2, NB, 128), jnp.float32),
            pltpu.VMEM((2, 2 * CH, HALF), jnp.bfloat16),
            pltpu.VMEM((WIN, NB, CH, 128), jnp.bfloat16),
            pltpu.VMEM((WIN, 4, 8, CH, 128), jnp.bfloat16),
            pltpu.VMEM((4, 2 * CH, ROUNDS * CH), jnp.float32),
            pltpu.VMEM((4, 4) + piece, jnp.float32),
            pltpu.VMEM((4, 4) + piece, jnp.bfloat16),
            pltpu.VMEM((NB,) + piece, jnp.float32),
            pltpu.VMEM((NB,) + piece, jnp.bfloat16),
            pltpu.VMEM((16, 8, NFFT), jnp.float32),
            dma, dma, dma, dma, dma((16,)), dma((16,)),
            dma((WIN, 16)), dma((WIN, 4, 4)), dma((WIN, 4, 4)), dma((WIN, 4, 4)), dma((2, 4, 4)), dma((2, NB)),
            pltpu.SemaphoreType.REGULAR((5,)),
        ],
        compiler_params=pltpu.CompilerParams(
            collective_id=0, has_side_effects=True, vmem_limit_bytes=60 * 1024 * 1024
        ),
        cost_estimate=pl.CostEstimate(flops=8_000_000_000, bytes_accessed=16_000_000, transcendentals=1_000_000),
    )(traces, offsets, tables)


def solution(mesh):
    return jax.shard_map(
        per_device,
        mesh=mesh,
        in_specs=(P("chan", "tm"), P("tm")),
        out_specs=P(None, None, ("chan", "tm"), None),
        check_vma=False,
    )
```

```python
import functools
import math

import jax
import jax.numpy as jnp
import numpy as np
from jax import lax
from jax.experimental import pallas as pl
from jax.experimental.pallas import tpu as pltpu
from jax.sharding import PartitionSpec as P

NFFT = 2048
HALF = 1024
BAND = 64
SEG = 4096
WIN = 4
ROUNDS = 4
NB = 16
CH = 128
WINDOWS = 32
MESH = pl.DeviceIdType.MESH
FOLD = (((4, 7, 3), range(0, 6)), ((4, 0, 3), range(6, 12)), ((4, 5, 1, 2, 3), range(12, 16)))
FOLD_ORDER = (12, 0, 6, 13, 1, 7, 14, 2, 8, 15, 3, 9, 4, 10, 5, 11)
FAR_FIRST = (
    (2, 2), (2, 0), (0, 2), (2, 1), (3, 2), (2, 3), (1, 2), (1, 1), (3, 3), (1, 3), (3, 1), (1, 0), (3, 0), (0, 1), (0, 3),
)


def fourier_tables():
    position = np.arange(HALF, dtype=np.int64)[:, None]
    inner = np.arange(BAND // 2, dtype=np.int64)
    tables = []
    for parity in range(2):
        bins, imag = [], []
        for group in range(NB // 2):
            first, second = (group, group + 8) if parity == 0 else (group + 8, group)
            for is_imag in (False, True):
                for band in (first, second):
                    bins.append(band * BAND + 2 * inner + parity)
                    imag.append(np.full(inner.shape, is_imag))
        bins, imag = np.concatenate(bins)[None, :], np.concatenate(imag)[None, :]
        angle = (position * bins % NFFT).astype(np.float64) * (2.0 * math.pi / NFFT)
        tables.append(np.where(imag, -np.sin(angle), np.cos(angle)))
    table = np.stack(tables)
    high = table.astype(jnp.bfloat16)
    low = (table - high.astype(np.float64)).astype(jnp.bfloat16)
    return np.stack([high, low])


def kernel(
    traces, offsets, tables, out,
    ext, tab, turns, split, white, rec, acc, own_out, far_out, own_in, far_in,
    relay, load_sem, tab_sem, halo_send, halo_recv, fold_send, fold_recv, b_send, b_recv, c_send, c_recv, d_send, d_recv, known,
):
    chan, tm = lax.axis_index("chan"), lax.axis_index("tm")
    zl, x, core = chan // 8, chan // 2 % 4, chan % 2
    zh, y = tm // 4, tm % 4
    block = chan % 8
    band = 4 * x + y
    plane = zl * 8
    sibling = (chan + 1 - 2 * core, tm)
    following = jnp.where(core == 0, chan + 1, (zl + 1) % 4 * 8 + 2 * x)
    preceding = jnp.where(core == 0, (zl + 3) % 4 * 8 + 2 * x + 1, chan - 1)

    def x_peer(step):
        return (plane + (x + step) % 4 * 2 + core, tm)

    def y_peer(step):
        return (chan, zh * 4 + (y + step) % 4)

    partner = (chan, (1 - zh) * 4 + y)

    barrier = pltpu.get_barrier_semaphore()
    for step in range(1, 4):
        pl.semaphore_signal(barrier, inc=1, device_id=x_peer(step), device_id_type=MESH)
        pl.semaphore_signal(barrier, inc=1, device_id=y_peer(step), device_id_type=MESH)
    pl.semaphore_signal(barrier, inc=1, device_id=partner, device_id_type=MESH)
    pl.semaphore_signal(barrier, inc=1, device_id=(following, tm), device_id_type=MESH)
    pl.semaphore_signal(barrier, inc=1, device_id=(preceding, tm), device_id_type=MESH)

    pl.semaphore_wait(barrier, 9)

    halo = pltpu.make_async_remote_copy(
        src_ref=traces.at[:, pl.ds(0, NFFT)],
        dst_ref=ext.at[:, pl.ds(SEG, NFFT)],
        send_sem=halo_send,
        recv_sem=halo_recv,
        device_id=(chan, jnp.maximum(tm - 1, 0)),
        device_id_type=MESH,
    )
    direct_out = jnp.logical_and(tm > 0, tm != 4)
    direct_in = jnp.logical_and(tm < 7, tm != 3)

    def fold_copy(path, piece, leg):
        first, last = leg == 0, leg == len(path) - 2
        rows = pl.ds(8 * piece, 8)
        return pltpu.make_async_remote_copy(
            src_ref=traces.at[rows, pl.ds(0, NFFT)] if first else relay.at[piece],
            dst_ref=ext.at[rows, pl.ds(SEG, NFFT)] if last else relay.at[piece],
            send_sem=fold_send.at[piece],
            recv_sem=fold_recv.at[piece],
            device_id=(chan, jnp.int32(path[leg + 1])),
            device_id_type=MESH,
        )

    @pl.when(direct_out)
    def _():
        halo.start()

    @pl.when(tm == 4)
    def _():
        for piece in FOLD_ORDER:
            path = next(path for path, pieces in FOLD if piece in pieces)
            fold_copy(path, piece, 0).start()

    load = pltpu.make_async_copy(traces, ext.at[:, pl.ds(0, SEG)], load_sem)
    load.start()
    table_load = pltpu.make_async_copy(tables, tab, tab_sem)
    table_load.start()

    for step in range(1, 4):
        pl.semaphore_signal(known.at[0], inc=1, device_id=y_peer(step), device_id_type=MESH)
    pl.semaphore_wait(known.at[0], 3)
    pl.semaphore_signal(known.at[1], inc=1, device_id=sibling, device_id_type=MESH)
    pl.semaphore_wait(known.at[1], 1)
    pl.semaphore_signal(known.at[2], inc=1, device_id=partner, device_id_type=MESH)
    pl.semaphore_wait(known.at[2], 1)

    @pl.when(tm == 7)
    def _():
        ext[:, pl.ds(SEG, NFFT)] = jnp.zeros((CH, NFFT), jnp.float32)

    column = lax.broadcasted_iota(jnp.int32, (NB, 128), 1)
    row = lax.broadcasted_iota(jnp.int32, (NB, 128), 0)
    swapped = row // 8
    frequency = row * BAND + 2 * (column % 32) + (column // 32 + swapped) % 2
    for w in range(WIN):
        angle = (frequency * offsets[w] % NFFT).astype(jnp.float32) * (2.0 * math.pi / NFFT)
        turns[w, 0] = jnp.cos(angle)
        turns[w, 1] = jnp.where(column < 64, -1.0, 1.0) * jnp.sin(angle)

    load.wait()
    table_load.wait()

    for path, pieces in FOLD:
        for leg in range(1, len(path) - 1):

            @pl.when(tm == path[leg])
            def _():
                for piece in pieces:
                    fold_copy(path, piece, leg - 1).wait_recv()
                    fold_copy(path, piece, leg).start()

    @pl.when(direct_in)
    def _():
        halo.wait_recv()

    @pl.when(tm == 3)
    def _():
        for path, pieces in FOLD:
            for piece in pieces:
                fold_copy(path, piece, len(path) - 2).wait_recv()

    for step in range(1, 4):
        pl.semaphore_signal(known.at[3], inc=1, device_id=y_peer(step), device_id_type=MESH)
    pl.semaphore_wait(known.at[3], 3)

    lane = lax.broadcasted_iota(jnp.int32, (CH, 128), 1)
    even_quarter = lane // 32 % 2 == 0
    to_mine = block // 4 == core

    def b_copy(w, dx, dy):
        to_x, to_y = (x + dx) % 4, (y + dy) % 4
        return pltpu.make_async_remote_copy(
            src_ref=white.at[w, to_x * 4 + to_y],
            dst_ref=rec.at[w, y, 4 + block % 4],
            send_sem=b_send.at[w, dx * 4 + dy],
            recv_sem=b_recv.at[w, y, block % 4],
            device_id=(plane + to_x * 2 + block // 4, zh * 4 + to_y),
            device_id_type=MESH,
        )

    def transform(w, carry):
        start = offsets[w]
        parts = []
        for k in range(16):
            place = lane + 128 * k
            near, middle, far = (ext[:, pl.ds(NFFT * part + 128 * k, 128)] for part in range(3))
            parts.append(jnp.where(place >= start, near, jnp.where(place >= start - NFFT, middle, far)))
        mean = jnp.sum(functools.reduce(jnp.add, parts), axis=1, keepdims=True) * (1.0 / NFFT)
        parts = [part - mean for part in parts]
        power = jnp.sum(functools.reduce(jnp.add, [part * part for part in parts]), axis=1, keepdims=True)
        scale = lax.rsqrt(power * (1.0 / NFFT) + 1e-06)
        parts = [part * scale for part in parts]
        for k in range(8):
            for parity in range(2):
                value = parts[k] + parts[k + 8] if parity == 0 else parts[k] - parts[k + 8]
                high = value.astype(jnp.bfloat16)
                split[parity, pl.ds(0, CH), pl.ds(128 * k, 128)] = high
                split[parity, pl.ds(CH, CH), pl.ds(128 * k, 128)] = (value - high.astype(jnp.float32)).astype(jnp.bfloat16)
        for quarter in range(4):
            columns = pl.ds(256 * quarter, 256)
            both = []
            for parity in range(2):
                main = jnp.dot(split[parity], tab[0, parity, :, columns], preferred_element_type=jnp.float32)
                rest = jnp.dot(split[parity, pl.ds(0, CH), :], tab[1, parity, :, columns], preferred_element_type=jnp.float32)
                both.append(main[:CH] + main[CH:] + rest)
            for group in range(2):
                j = 2 * quarter + group
                even, odd = (part[:, 128 * group : 128 * group + 128] for part in both)
                for which, tile in ((j, jnp.where(even_quarter, even, odd)), (j + 8, jnp.where(even_quarter, odd, even))):
                    square = tile * tile
                    size = jnp.sqrt(square + pltpu.roll(square, 64, 1))
                    level = jnp.sum(size, axis=1, keepdims=True) * (0.5 / BAND)
                    tile = tile * (1.0 / (level + 1e-06))
                    straight = turns[w, 0, which : which + 1, :]
                    across = turns[w, 1, which : which + 1, :]
                    white[w, which] = (tile * straight + pltpu.roll(tile, 64, 1) * across).astype(jnp.bfloat16)
        for dx, dy in FAR_FIRST:
            b_copy(w, dx, dy).start()

        @pl.when(to_mine)
        def _():
            rec[w, y, 4 + block % 4] = white[w, band]

        @pl.when(jnp.logical_not(to_mine))
        def _():
            b_copy(w, 0, 0).start()

        return carry

    lax.fori_loop(0, WIN, transform, 0)

    def c_copy(w, from_y, i):
        return pltpu.make_async_remote_copy(
            src_ref=rec.at[w, from_y, 4 + i],
            dst_ref=rec.at[w, from_y, i],
            send_sem=c_send.at[w, from_y, i],
            recv_sem=c_recv.at[w, from_y, i],
            device_id=(following, tm),
            device_id_type=MESH,
        )

    def forward(w):
        for turn in (2, 3, 1, 0):
            from_y = (y + turn) % 4
            for i in range(4):
                arrival = pltpu.make_async_remote_copy(
                    src_ref=white.at[w, 0],
                    dst_ref=rec.at[w, from_y, 4 + i],
                    send_sem=b_send.at[w, 0],
                    recv_sem=b_recv.at[w, from_y, i],
                    device_id=sibling,
                    device_id_type=MESH,
                )
                mine = jnp.logical_and(block == 4 * core + i, y == from_y)

                @pl.when(jnp.logical_not(mine))
                def _():
                    arrival.wait_recv()

                c_copy(w, from_y, i).start()

    sign = jnp.where(lane < 64, 1.0, -1.0)

    def cross(w, i):
        own = [rec[w, from_y, 4 + i] for from_y in range(4)]
        turned = [(pltpu.roll(tile.astype(jnp.float32), 64, 1) * sign).astype(jnp.bfloat16) for tile in own]
        left = jnp.concatenate([jnp.concatenate(own, axis=1), jnp.concatenate(turned, axis=1)], axis=0)
        right = jnp.concatenate([rec[w, from_y, pl.ds(i, 4)].reshape(4 * CH, 128) for from_y in range(4)], axis=1)
        return lax.dot_general(left, right, (((1,), (1,)), ((), ())), preferred_element_type=jnp.float32)

    def add_window(w):
        for from_y in range(4):
            for i in range(4):
                c_copy(w, from_y, i).wait_recv()

        def one(i, carry):
            @pl.when(w == 0)
            def _():
                acc[i] = cross(w, i)

            @pl.when(w > 0)
            def _():
                acc[i] += cross(w, i)

            return carry

        lax.fori_loop(0, 4, one, 0)

    def exchange(w, carry):
        forward(w)

        @pl.when(w > 0)
        def _():
            add_window(w - 1)

        return carry

    lax.fori_loop(0, WIN, exchange, 0)
    for from_y in range(4):
        for i in range(4):
            c_copy(WIN - 1, from_y, i).wait_recv()

    norm = 1.0 / math.sqrt(WINDOWS * BAND)

    def far_copy(i, dy):
        to_y = (y + dy) % 4
        return pltpu.make_async_remote_copy(
            src_ref=far_out.at[i, to_y],
            dst_ref=far_in.at[band],
            send_sem=d_send.at[0, i, dy],
            recv_sem=d_recv.at[0, band],
            device_id=(plane + 4 * core + i, (1 - zh) * 4 + to_y),
            device_id_type=MESH,
        )

    def own_copy(i, dy):
        to_y = (y + dy) % 4
        return pltpu.make_async_remote_copy(
            src_ref=own_out.at[i, to_y],
            dst_ref=own_in.at[band],
            send_sem=d_send.at[1, i, dy],
            recv_sem=d_recv.at[1, band],
            device_id=(plane + 4 * core + i, zh * 4 + to_y),
            device_id_type=MESH,
        )

    def give(step, carry):
        i = (step + x) % 4
        acc[i] = (acc[i] + cross(WIN - 1, i)) * norm
        for to_y in range(4):
            for r in range(ROUNDS):
                for part in range(2):
                    columns = pl.ds(128 * (ROUNDS - 1 - r), 128)
                    far_rows = pl.ds(pl.multiple_of(part * CH + 64 * (1 - zh) + 16 * to_y, 16), 16)
                    far_out[i, to_y, r, part] = acc[i, far_rows, columns].astype(jnp.bfloat16)
                    own_rows = pl.ds(pl.multiple_of(part * CH + 64 * zh + 16 * to_y, 16), 16)
                    own_out[i, to_y, r, part] = acc[i, own_rows, columns]
        for dy in range(4):
            far_copy(i, dy).start()
        for dy in range(4):
            if dy == 0:
                mine = block == 4 * core + i

                @pl.when(mine)
                def _():
                    own_in[band] = own_out[i, y]

                @pl.when(jnp.logical_not(mine))
                def _():
                    own_copy(i, 0).start()
            else:
                own_copy(i, dy).start()
        return carry

    for step in range(1, 4):
        pl.semaphore_signal(known.at[4], inc=1, device_id=y_peer(step), device_id_type=MESH)
        pl.semaphore_signal(known.at[4], inc=1, device_id=x_peer(step), device_id_type=MESH)
    pl.semaphore_signal(known.at[4], inc=1, device_id=partner, device_id_type=MESH)
    pl.semaphore_signal(known.at[4], inc=1, device_id=sibling, device_id_type=MESH)
    pl.semaphore_wait(known.at[4], 8)
    lax.fori_loop(0, 4, give, 0)

    def take(m, carry):
        arrival = pltpu.make_async_remote_copy(
            src_ref=own_out.at[0, 0], dst_ref=own_in.at[m], send_sem=d_send.at[1, 0, 0],
            recv_sem=d_recv.at[1, m], device_id=sibling, device_id_type=MESH,
        )
        mine = jnp.logical_and(m == band, to_mine)

        @pl.when(jnp.logical_not(mine))
        def _():
            arrival.wait_recv()

        pltpu.make_async_remote_copy(
            src_ref=far_out.at[0, 0], dst_ref=far_in.at[m], send_sem=d_send.at[0, 0, 0],
            recv_sem=d_recv.at[0, m], device_id=sibling, device_id_type=MESH,
        ).wait_recv()
        for r in range(ROUNDS):
            for part in range(2):
                out[r, part * NB + m] = own_in[m, r, part] + far_in[m, r, part].astype(jnp.float32)
        return carry

    lax.fori_loop(0, NB, take, 0)

    @pl.when(direct_out)
    def _():
        halo.wait_send()

    for path, pieces in FOLD:
        for leg in range(len(path) - 1):

            @pl.when(tm == path[leg])
            def _():
                for piece in pieces:
                    fold_copy(path, piece, leg).wait_send()

    def b_left(w, carry):
        for dx in range(4):
            for dy in range(4):
                if dx == 0 and dy == 0:

                    @pl.when(jnp.logical_not(to_mine))
                    def _():
                        b_copy(w, 0, 0).wait_send()
                else:
                    b_copy(w, dx, dy).wait_send()
        for from_y in range(4):
            for i in range(4):
                c_copy(w, from_y, i).wait_send()
        return carry

    lax.fori_loop(0, WIN, b_left, 0)

    def d_left(i, carry):
        for dy in range(4):
            far_copy(i, dy).wait_send()
            if dy == 0:

                @pl.when(block != 4 * core + i)
                def _():
                    own_copy(i, 0).wait_send()
            else:
                own_copy(i, dy).wait_send()
        return carry

    lax.fori_loop(0, 4, d_left, 0)


def per_device(traces, offsets):
    tables = jnp.asarray(fourier_tables())
    dma = pltpu.SemaphoreType.DMA
    piece = (ROUNDS, 2, 16, CH)
    return pl.pallas_call(
        kernel,
        out_shape=jax.ShapeDtypeStruct((ROUNDS, 2 * NB, 16, CH), jnp.float32),
        in_specs=[
            pl.BlockSpec(memory_space=pltpu.HBM),
            pl.BlockSpec(memory_space=pltpu.SMEM),
            pl.BlockSpec(memory_space=pltpu.HBM),
        ],
        out_specs=pl.BlockSpec(memory_space=pltpu.VMEM),
        scratch_shapes=[
            pltpu.VMEM((CH, SEG + NFFT), jnp.float32),
            pltpu.VMEM((2, 2, HALF, HALF), jnp.bfloat16),
            pltpu.VMEM((WIN, 2, NB, 128), jnp.float32),
            pltpu.VMEM((2, 2 * CH, HALF), jnp.bfloat16),
            pltpu.VMEM((WIN, NB, CH, 128), jnp.bfloat16),
            pltpu.VMEM((WIN, 4, 8, CH, 128), jnp.bfloat16),
            pltpu.VMEM((4, 2 * CH, ROUNDS * CH), jnp.float32),
            pltpu.VMEM((4, 4) + piece, jnp.float32),
            pltpu.VMEM((4, 4) + piece, jnp.bfloat16),
            pltpu.VMEM((NB,) + piece, jnp.float32),
            pltpu.VMEM((NB,) + piece, jnp.bfloat16),
            pltpu.VMEM((16, 8, NFFT), jnp.float32),
            dma, dma, dma, dma, dma((16,)), dma((16,)),
            dma((WIN, 16)), dma((WIN, 4, 4)), dma((WIN, 4, 4)), dma((WIN, 4, 4)), dma((2, 4, 4)), dma((2, NB)),
            pltpu.SemaphoreType.REGULAR((5,)),
        ],
        compiler_params=pltpu.CompilerParams(
            collective_id=0, has_side_effects=True, vmem_limit_bytes=48 * 1024 * 1024
        ),
        cost_estimate=pl.CostEstimate(flops=8_000_000_000, bytes_accessed=16_000_000, transcendentals=1_000_000),
    )(traces, offsets, tables)


def solution(mesh):
    return jax.shard_map(
        per_device,
        mesh=mesh,
        in_specs=(P("chan", "tm"), P("tm")),
        out_specs=P(None, None, ("chan", "tm"), None),
        check_vma=False,
    )
```

```python
import functools
import math

import jax
import jax.numpy as jnp
import numpy as np
from jax import lax
from jax.experimental import pallas as pl
from jax.experimental.pallas import tpu as pltpu
from jax.sharding import PartitionSpec as P

NFFT = 2048
HALF = 1024
BAND = 64
SEG = 4096
WIN = 4
ROUNDS = 4
NB = 16
CH = 128
WINDOWS = 32
MESH = pl.DeviceIdType.MESH
FOLD = (((4, 7, 3), range(0, 6)), ((4, 0, 3), range(6, 12)), ((4, 5, 1, 2, 3), range(12, 16)))
FOLD_ORDER = (12, 0, 6, 13, 1, 7, 14, 2, 8, 15, 3, 9, 4, 10, 5, 11)
FAR_FIRST = (
    (2, 2), (2, 0), (0, 2), (2, 1), (3, 2), (2, 3), (1, 2), (1, 1), (3, 3), (1, 3), (3, 1), (1, 0), (3, 0), (0, 1), (0, 3),
)


def fourier_tables():
    position = np.arange(HALF, dtype=np.int64)[:, None]
    inner = np.arange(BAND // 2, dtype=np.int64)
    tables = []
    for parity in range(2):
        bins, imag = [], []
        for group in range(NB // 2):
            first, second = (group, group + 8) if parity == 0 else (group + 8, group)
            for is_imag in (False, True):
                for band in (first, second):
                    bins.append(band * BAND + 2 * inner + parity)
                    imag.append(np.full(inner.shape, is_imag))
        bins, imag = np.concatenate(bins)[None, :], np.concatenate(imag)[None, :]
        angle = (position * bins % NFFT).astype(np.float64) * (2.0 * math.pi / NFFT)
        tables.append(np.where(imag, -np.sin(angle), np.cos(angle)))
    table = np.stack(tables)
    high = table.astype(jnp.bfloat16)
    low = (table - high.astype(np.float64)).astype(jnp.bfloat16)
    return np.stack([high, low])


def kernel(
    traces, offsets_in, tables, out,
    offsets, ext, tab, turns, split, white, rec, acc, own_out, far_out, own_in, far_in,
    relay, offset_sem, load_sem, tab_sem, halo_send, halo_recv, fold_send, fold_recv, b_send, b_recv, c_send, c_recv, d_send, d_recv, known,
):
    chan, tm = lax.axis_index("chan"), lax.axis_index("tm")
    zl, x, core = chan // 8, chan // 2 % 4, chan % 2
    zh, y = tm // 4, tm % 4
    block = chan % 8
    band = 4 * x + y
    plane = zl * 8
    sibling = (chan + 1 - 2 * core, tm)
    following = jnp.where(core == 0, chan + 1, (zl + 1) % 4 * 8 + 2 * x)
    preceding = jnp.where(core == 0, (zl + 3) % 4 * 8 + 2 * x + 1, chan - 1)

    def x_peer(step):
        return (plane + (x + step) % 4 * 2 + core, tm)

    def y_peer(step):
        return (chan, zh * 4 + (y + step) % 4)

    partner = (chan, (1 - zh) * 4 + y)

    barrier = pltpu.get_barrier_semaphore()
    for step in range(1, 4):
        pl.semaphore_signal(barrier, inc=1, device_id=x_peer(step), device_id_type=MESH)
        pl.semaphore_signal(barrier, inc=1, device_id=y_peer(step), device_id_type=MESH)
    pl.semaphore_signal(barrier, inc=1, device_id=partner, device_id_type=MESH)
    pl.semaphore_signal(barrier, inc=1, device_id=(following, tm), device_id_type=MESH)
    pl.semaphore_signal(barrier, inc=1, device_id=(preceding, tm), device_id_type=MESH)

    pl.semaphore_wait(barrier, 9)

    halo = pltpu.make_async_remote_copy(
        src_ref=traces.at[:, pl.ds(0, NFFT)],
        dst_ref=ext.at[:, pl.ds(SEG, NFFT)],
        send_sem=halo_send,
        recv_sem=halo_recv,
        device_id=(chan, jnp.maximum(tm - 1, 0)),
        device_id_type=MESH,
    )
    direct_out = jnp.logical_and(tm > 0, tm != 4)
    direct_in = jnp.logical_and(tm < 7, tm != 3)

    def fold_copy(path, piece, leg):
        first, last = leg == 0, leg == len(path) - 2
        rows = pl.ds(8 * piece, 8)
        return pltpu.make_async_remote_copy(
            src_ref=traces.at[rows, pl.ds(0, NFFT)] if first else relay.at[piece],
            dst_ref=ext.at[rows, pl.ds(SEG, NFFT)] if last else relay.at[piece],
            send_sem=fold_send.at[piece],
            recv_sem=fold_recv.at[piece],
            device_id=(chan, jnp.int32(path[leg + 1])),
            device_id_type=MESH,
        )

    @pl.when(direct_out)
    def _():
        halo.start()

    @pl.when(tm == 4)
    def _():
        for piece in FOLD_ORDER:
            path = next(path for path, pieces in FOLD if piece in pieces)
            fold_copy(path, piece, 0).start()

    load = pltpu.make_async_copy(traces, ext.at[:, pl.ds(0, SEG)], load_sem)
    load.start()
    offset_load = pltpu.make_async_copy(offsets_in, offsets, offset_sem)
    offset_load.start()
    table_load = pltpu.make_async_copy(tables, tab, tab_sem)
    table_load.start()

    for step in range(1, 4):
        pl.semaphore_signal(known.at[0], inc=1, device_id=y_peer(step), device_id_type=MESH)
    pl.semaphore_wait(known.at[0], 3)
    pl.semaphore_signal(known.at[1], inc=1, device_id=sibling, device_id_type=MESH)
    pl.semaphore_wait(known.at[1], 1)
    pl.semaphore_signal(known.at[2], inc=1, device_id=partner, device_id_type=MESH)
    pl.semaphore_wait(known.at[2], 1)

    @pl.when(tm == 7)
    def _():
        ext[:, pl.ds(SEG, NFFT)] = jnp.zeros((CH, NFFT), jnp.float32)

    column = lax.broadcasted_iota(jnp.int32, (NB, 128), 1)
    row = lax.broadcasted_iota(jnp.int32, (NB, 128), 0)
    swapped = row // 8
    frequency = row * BAND + 2 * (column % 32) + (column // 32 + swapped) % 2
    offset_load.wait()
    for w in range(WIN):
        angle = (frequency * offsets[w] % NFFT).astype(jnp.float32) * (2.0 * math.pi / NFFT)
        turns[w, 0] = jnp.cos(angle)
        turns[w, 1] = jnp.where(column < 64, -1.0, 1.0) * jnp.sin(angle)

    load.wait()
    table_load.wait()

    for path, pieces in FOLD:
        for leg in range(1, len(path) - 1):

            @pl.when(tm == path[leg])
            def _():
                for piece in pieces:
                    fold_copy(path, piece, leg - 1).wait_recv()
                    fold_copy(path, piece, leg).start()

    @pl.when(direct_in)
    def _():
        halo.wait_recv()

    @pl.when(tm == 3)
    def _():
        for path, pieces in FOLD:
            for piece in pieces:
                fold_copy(path, piece, len(path) - 2).wait_recv()

    for step in range(1, 4):
        pl.semaphore_signal(known.at[3], inc=1, device_id=y_peer(step), device_id_type=MESH)
    pl.semaphore_wait(known.at[3], 3)

    lane = lax.broadcasted_iota(jnp.int32, (CH, 128), 1)
    even_quarter = lane // 32 % 2 == 0
    to_mine = block // 4 == core

    def b_copy(w, dx, dy):
        to_x, to_y = (x + dx) % 4, (y + dy) % 4
        return pltpu.make_async_remote_copy(
            src_ref=white.at[w, to_x * 4 + to_y],
            dst_ref=rec.at[w, y, 4 + block % 4],
            send_sem=b_send.at[w, dx * 4 + dy],
            recv_sem=b_recv.at[w, y, block % 4],
            device_id=(plane + to_x * 2 + block // 4, zh * 4 + to_y),
            device_id_type=MESH,
        )

    def transform(w, carry):
        start = offsets[w]
        parts = []
        for k in range(16):
            place = lane + 128 * k
            near, middle, far = (ext[:, pl.ds(NFFT * part + 128 * k, 128)] for part in range(3))
            parts.append(jnp.where(place >= start, near, jnp.where(place >= start - NFFT, middle, far)))
        mean = jnp.sum(functools.reduce(jnp.add, parts), axis=1, keepdims=True) * (1.0 / NFFT)
        parts = [part - mean for part in parts]
        power = jnp.sum(functools.reduce(jnp.add, [part * part for part in parts]), axis=1, keepdims=True)
        scale = lax.rsqrt(power * (1.0 / NFFT) + 1e-06)
        parts = [part * scale for part in parts]
        for k in range(8):
            for parity in range(2):
                value = parts[k] + parts[k + 8] if parity == 0 else parts[k] - parts[k + 8]
                high = value.astype(jnp.bfloat16)
                split[parity, pl.ds(0, CH), pl.ds(128 * k, 128)] = high
                split[parity, pl.ds(CH, CH), pl.ds(128 * k, 128)] = (value - high.astype(jnp.float32)).astype(jnp.bfloat16)
        for quarter in range(4):
            columns = pl.ds(256 * quarter, 256)
            both = []
            for parity in range(2):
                main = jnp.dot(split[parity], tab[0, parity, :, columns], preferred_element_type=jnp.float32)
                rest = jnp.dot(split[parity, pl.ds(0, CH), :], tab[1, parity, :, columns], preferred_element_type=jnp.float32)
                both.append(main[:CH] + main[CH:] + rest)
            for group in range(2):
                j = 2 * quarter + group
                even, odd = (part[:, 128 * group : 128 * group + 128] for part in both)
                for which, tile in ((j, jnp.where(even_quarter, even, odd)), (j + 8, jnp.where(even_quarter, odd, even))):
                    square = tile * tile
                    size = jnp.sqrt(square + pltpu.roll(square, 64, 1))
                    level = jnp.sum(size, axis=1, keepdims=True) * (0.5 / BAND)
                    tile = tile * (1.0 / (level + 1e-06))
                    straight = turns[w, 0, which : which + 1, :]
                    across = turns[w, 1, which : which + 1, :]
                    white[w, which] = (tile * straight + pltpu.roll(tile, 64, 1) * across).astype(jnp.bfloat16)
        for dx, dy in FAR_FIRST:
            b_copy(w, dx, dy).start()

        @pl.when(to_mine)
        def _():
            rec[w, y, 4 + block % 4] = white[w, band]

        @pl.when(jnp.logical_not(to_mine))
        def _():
            b_copy(w, 0, 0).start()

        return carry

    lax.fori_loop(0, WIN, transform, 0)

    def c_copy(w, from_y, i):
        return pltpu.make_async_remote_copy(
            src_ref=rec.at[w, from_y, 4 + i],
            dst_ref=rec.at[w, from_y, i],
            send_sem=c_send.at[w, from_y, i],
            recv_sem=c_recv.at[w, from_y, i],
            device_id=(following, tm),
            device_id_type=MESH,
        )

    def forward(w):
        for turn in (2, 3, 1, 0):
            from_y = (y + turn) % 4
            for i in range(4):
                arrival = pltpu.make_async_remote_copy(
                    src_ref=white.at[w, 0],
                    dst_ref=rec.at[w, from_y, 4 + i],
                    send_sem=b_send.at[w, 0],
                    recv_sem=b_recv.at[w, from_y, i],
                    device_id=sibling,
                    device_id_type=MESH,
                )
                mine = jnp.logical_and(block == 4 * core + i, y == from_y)

                @pl.when(jnp.logical_not(mine))
                def _():
                    arrival.wait_recv()

                c_copy(w, from_y, i).start()

    sign = jnp.where(lane < 64, 1.0, -1.0)

    def cross(w, i):
        own = [rec[w, from_y, 4 + i] for from_y in range(4)]
        turned = [(pltpu.roll(tile.astype(jnp.float32), 64, 1) * sign).astype(jnp.bfloat16) for tile in own]
        left = jnp.concatenate([jnp.concatenate(own, axis=1), jnp.concatenate(turned, axis=1)], axis=0)
        right = jnp.concatenate([rec[w, from_y, pl.ds(i, 4)].reshape(4 * CH, 128) for from_y in range(4)], axis=1)
        return lax.dot_general(left, right, (((1,), (1,)), ((), ())), preferred_element_type=jnp.float32)

    def add_window(w):
        for from_y in range(4):
            for i in range(4):
                c_copy(w, from_y, i).wait_recv()

        def one(i, carry):
            @pl.when(w == 0)
            def _():
                acc[i] = cross(w, i)

            @pl.when(w > 0)
            def _():
                acc[i] += cross(w, i)

            return carry

        lax.fori_loop(0, 4, one, 0)

    def exchange(w, carry):
        forward(w)

        @pl.when(w > 0)
        def _():
            add_window(w - 1)

        return carry

    lax.fori_loop(0, WIN, exchange, 0)
    for from_y in range(4):
        for i in range(4):
            c_copy(WIN - 1, from_y, i).wait_recv()

    norm = 1.0 / math.sqrt(WINDOWS * BAND)

    def far_copy(i, dy):
        to_y = (y + dy) % 4
        return pltpu.make_async_remote_copy(
            src_ref=far_out.at[i, to_y],
            dst_ref=far_in.at[band],
            send_sem=d_send.at[0, i, dy],
            recv_sem=d_recv.at[0, band],
            device_id=(plane + 4 * core + i, (1 - zh) * 4 + to_y),
            device_id_type=MESH,
        )

    def own_copy(i, dy):
        to_y = (y + dy) % 4
        return pltpu.make_async_remote_copy(
            src_ref=own_out.at[i, to_y],
            dst_ref=own_in.at[band],
            send_sem=d_send.at[1, i, dy],
            recv_sem=d_recv.at[1, band],
            device_id=(plane + 4 * core + i, zh * 4 + to_y),
            device_id_type=MESH,
        )

    def give(step, carry):
        i = (step + x) % 4
        acc[i] = (acc[i] + cross(WIN - 1, i)) * norm
        for to_y in range(4):
            for r in range(ROUNDS):
                for part in range(2):
                    columns = pl.ds(128 * (ROUNDS - 1 - r), 128)
                    far_rows = pl.ds(pl.multiple_of(part * CH + 64 * (1 - zh) + 16 * to_y, 16), 16)
                    far_out[i, to_y, r, part] = acc[i, far_rows, columns].astype(jnp.bfloat16)
                    own_rows = pl.ds(pl.multiple_of(part * CH + 64 * zh + 16 * to_y, 16), 16)
                    own_out[i, to_y, r, part] = acc[i, own_rows, columns]
        for dy in range(4):
            far_copy(i, dy).start()
        for dy in range(4):
            if dy == 0:
                mine = block == 4 * core + i

                @pl.when(mine)
                def _():
                    own_in[band] = own_out[i, y]

                @pl.when(jnp.logical_not(mine))
                def _():
                    own_copy(i, 0).start()
            else:
                own_copy(i, dy).start()
        return carry

    for step in range(1, 4):
        pl.semaphore_signal(known.at[4], inc=1, device_id=y_peer(step), device_id_type=MESH)
    pl.semaphore_signal(known.at[4], inc=1, device_id=partner, device_id_type=MESH)
    pl.semaphore_signal(known.at[4], inc=1, device_id=sibling, device_id_type=MESH)
    pl.semaphore_wait(known.at[4], 5)
    lax.fori_loop(0, 4, give, 0)

    def take(m, carry):
        arrival = pltpu.make_async_remote_copy(
            src_ref=own_out.at[0, 0], dst_ref=own_in.at[m], send_sem=d_send.at[1, 0, 0],
            recv_sem=d_recv.at[1, m], device_id=sibling, device_id_type=MESH,
        )
        mine = jnp.logical_and(m == band, to_mine)

        @pl.when(jnp.logical_not(mine))
        def _():
            arrival.wait_recv()

        pltpu.make_async_remote_copy(
            src_ref=far_out.at[0, 0], dst_ref=far_in.at[m], send_sem=d_send.at[0, 0, 0],
            recv_sem=d_recv.at[0, m], device_id=sibling, device_id_type=MESH,
        ).wait_recv()
        for r in range(ROUNDS):
            for part in range(2):
                out[r, part * NB + m] = own_in[m, r, part] + far_in[m, r, part].astype(jnp.float32)
        return carry

    lax.fori_loop(0, NB, take, 0)

    @pl.when(direct_out)
    def _():
        halo.wait_send()

    for path, pieces in FOLD:
        for leg in range(len(path) - 1):

            @pl.when(tm == path[leg])
            def _():
                for piece in pieces:
                    fold_copy(path, piece, leg).wait_send()

    def b_left(w, carry):
        for dx in range(4):
            for dy in range(4):
                if dx == 0 and dy == 0:

                    @pl.when(jnp.logical_not(to_mine))
                    def _():
                        b_copy(w, 0, 0).wait_send()
                else:
                    b_copy(w, dx, dy).wait_send()
        for from_y in range(4):
            for i in range(4):
                c_copy(w, from_y, i).wait_send()
        return carry

    lax.fori_loop(0, WIN, b_left, 0)

    def d_left(i, carry):
        for dy in range(4):
            far_copy(i, dy).wait_send()
            if dy == 0:

                @pl.when(block != 4 * core + i)
                def _():
                    own_copy(i, 0).wait_send()
            else:
                own_copy(i, dy).wait_send()
        return carry

    lax.fori_loop(0, 4, d_left, 0)


def per_device(traces, offsets):
    tables = jnp.asarray(fourier_tables())
    dma = pltpu.SemaphoreType.DMA
    piece = (ROUNDS, 2, 16, CH)
    return pl.pallas_call(
        kernel,
        out_shape=jax.ShapeDtypeStruct((ROUNDS, 2 * NB, 16, CH), jnp.float32),
        in_specs=[
            pl.BlockSpec(memory_space=pltpu.HBM),
            pl.BlockSpec(memory_space=pltpu.HBM),
            pl.BlockSpec(memory_space=pltpu.HBM),
        ],
        out_specs=pl.BlockSpec(memory_space=pltpu.VMEM),
        scratch_shapes=[
            pltpu.SMEM((WIN,), jnp.int32),
            pltpu.VMEM((CH, SEG + NFFT), jnp.float32),
            pltpu.VMEM((2, 2, HALF, HALF), jnp.bfloat16),
            pltpu.VMEM((WIN, 2, NB, 128), jnp.float32),
            pltpu.VMEM((2, 2 * CH, HALF), jnp.bfloat16),
            pltpu.VMEM((WIN, NB, CH, 128), jnp.bfloat16),
            pltpu.VMEM((WIN, 4, 8, CH, 128), jnp.bfloat16),
            pltpu.VMEM((4, 2 * CH, ROUNDS * CH), jnp.float32),
            pltpu.VMEM((4, 4) + piece, jnp.float32),
            pltpu.VMEM((4, 4) + piece, jnp.bfloat16),
            pltpu.VMEM((NB,) + piece, jnp.float32),
            pltpu.VMEM((NB,) + piece, jnp.bfloat16),
            pltpu.VMEM((16, 8, NFFT), jnp.float32),
            dma, dma, dma, dma, dma, dma((16,)), dma((16,)),
            dma((WIN, 16)), dma((WIN, 4, 4)), dma((WIN, 4, 4)), dma((WIN, 4, 4)), dma((2, 4, 4)), dma((2, NB)),
            pltpu.SemaphoreType.REGULAR((5,)),
        ],
        compiler_params=pltpu.CompilerParams(
            collective_id=0, has_side_effects=True, vmem_limit_bytes=48 * 1024 * 1024
        ),
        cost_estimate=pl.CostEstimate(flops=8_000_000_000, bytes_accessed=16_000_000, transcendentals=1_000_000),
    )(traces, offsets, tables)


def solution(mesh):
    return jax.shard_map(
        per_device,
        mesh=mesh,
        in_specs=(P("chan", "tm"), P("tm")),
        out_specs=P(None, None, ("chan", "tm"), None),
        check_vma=False,
    )
```
